256 devices in a mesh: leaf: 8 (over z), wide: 32 (over x, y, core).
Axes of the slice: x: 4, y: 4, z: 8, core: 2. Of those that a mesh axis runs over, the one named last changes fastest.
Arguments:
- points: float32 [64, 1048576], P(None, ('leaf', 'wide')), may hold values from -6 to 6
- leaf_basis: bfloat16 [1048576, 256], P(('leaf', 'wide')), may hold values from -0.25 to 0.25
- right_sides: bfloat16 [32, 1048576], P(None, ('leaf', 'wide')), may hold values from -6 to 6
- leaf_order: int32 [1048576], P(('leaf', 'wide')), may hold values from 0 to 4095, as said below
- local_up: bfloat16 [3584, 256, 256], P(('leaf', 'wide')), may hold values from -0.25 to 0.25
- local_down: bfloat16 [3584, 256, 256], P(('leaf', 'wide')), may hold values from -0.375 to 0.375
- local_links: bfloat16 [1792, 2, 256, 256], P(('leaf', 'wide')), may hold values from -0.109375 to 0.109375
- upper_nodes: bfloat16 [256, 8, 3, 256, 256], P(('leaf', 'wide')), as said below
Outputs:
- kernel_product: float32 [32, 1048576], P(None, ('leaf', 'wide'))
The draws below stay inside these ranges and needn't reach their ends.
Inputs may be any that keep to these rules, and one draw needn't show every extreme that they name: `leaf_order`: each aligned block of 4096 entries holds every value of 0 to 4095 once. upper_nodes[d, j] is the same for all devices d whose indices (leaf axis the slower) agree after dropping their lowest j bits: the upward matrix, downward matrix and sibling coupling of their common ancestor at height 3 + j.
All inputs are finite; a program needn't handle non-finite values.
Results may differ from the reference program's by a relative error of at most 0.002.
Values sent between devices are 32-bit elements; how exact they have to be, the bound alone decides.
A program may use at most 64 MiB of HBM per device.

```python
import jax
import jax.numpy as jnp
from jax import lax

LEAF = 512
RANK = 256
COLS = 32
DIMS = 64
LEAVES_DEV = 8
PTS_DEV = 4096
NPTS = 1048576
ALL_LEAVES = 2048
LOCAL_LEVELS = 3
CROSS_LEVELS = 8
DEVICES = 256


def draw_leaf_order(key, part):
    key = jax.random.fold_in(key, 5)
    blocks = jnp.arange(NPTS // PTS_DEV, dtype=jnp.int32)

    def one_block(index):
        return jax.random.permutation(jax.random.fold_in(key, index), PTS_DEV).astype(jnp.int32)
    return jax.vmap(one_block)(blocks).reshape(NPTS)


def draw_upper_nodes(key, part):
    key = jax.random.fold_in(key, 11)
    scales = jnp.array([(2.0 * RANK) ** (-0.5), RANK ** (-0.5), (11.0 * RANK) ** (-0.5)], jnp.float32)
    slots = []
    for tier in range(CROSS_LEVELS):
        number = DEVICES >> tier
        tier_key = jax.random.fold_in(key, tier)
        values = jax.random.normal(tier_key, (number, 3, RANK, RANK), jnp.float32)
        values = (values * scales[None, :, None, None]).astype(jnp.bfloat16)
        slots.append(jnp.repeat(values, 2 ** tier, axis=0))
    return jnp.stack(slots, axis=1)


def levels(stream_key, dims, split, smallest, largest):
    factor_of = 1.0
    for axis_at, blocks in split:
        steps = jax.random.uniform(jax.random.fold_in(jax.random.fold_in(stream_key, 6), axis_at), (blocks,), jnp.float32, smallest / len(split), largest / len(split))
        factor_of = factor_of * jnp.repeat(jnp.exp(steps), dims[axis_at] // blocks).reshape((-1,) + (1,) * (len(dims) - 1 - axis_at))
    return factor_of


def centred(rng, extent, deviation, limit, cuts=(), kind=jnp.bfloat16):
    entries = deviation * jax.random.normal(rng, extent, jnp.float32)
    if cuts:
        entries = entries * levels(rng, extent, cuts, -0.22, 0.18)
    return jnp.clip(entries, -limit, limit).astype(kind)


def setup_inputs(seed: int = 0) -> dict:
    arg_keys = jax.random.split(jax.random.key(seed), 9)
    points = centred(arg_keys[0], (DIMS, NPTS), 1.0, 6.0, ((1, 256),), jnp.float32)
    leaf_basis = centred(arg_keys[1], (NPTS, RANK), LEAF ** -0.5, 0.25, ((0, 256),))
    right_sides = centred(arg_keys[2], (COLS, NPTS), 1.0, 6.0, ((1, 256),))
    leaf_order = draw_leaf_order(jax.random.fold_in(arg_keys[8], 71), 0)
    local_up = centred(arg_keys[4], (DEVICES * (2 * LEAVES_DEV - 2), RANK, RANK), (2 * RANK) ** -0.5, 0.25, ((0, 256),))
    local_down = centred(arg_keys[5], (DEVICES * (2 * LEAVES_DEV - 2), RANK, RANK), RANK ** -0.5, 0.375, ((0, 256),))
    local_links = centred(arg_keys[6], (DEVICES * (LEAVES_DEV - 1), 2, RANK, RANK), (11 * RANK) ** -0.5, 0.109375, ((0, 256),))
    upper_nodes = draw_upper_nodes(jax.random.fold_in(arg_keys[8], 71), 0)
    return dict(points=points, leaf_basis=leaf_basis, right_sides=right_sides, leaf_order=leaf_order, local_up=local_up, local_down=local_down, local_links=local_links, upper_nodes=upper_nodes)


HIGHEST = lax.Precision.HIGHEST
RIDGE_TERM = 1.0


def kernel_blocks(coords):
    squares = jnp.sum(coords * coords, axis=0)
    inner_prod = jnp.einsum('dal,dam->alm', coords, coords, precision=HIGHEST)
    distance = squares[:, :, None] + squares[:, None, :] - 2.0 * inner_prod
    identity = jnp.eye(coords.shape[2], dtype=jnp.float32)
    blocks = jnp.exp(distance * (-2.0 / coords.shape[0])) + RIDGE_TERM * identity
    return lax.optimization_barrier(blocks.astype(jnp.bfloat16))


def rounded(values):
    return lax.optimization_barrier(values.astype(jnp.bfloat16)).astype(jnp.float32)


def batched(values, matrices):
    return jnp.einsum('nkr,nrs->nks', values, matrices.astype(jnp.float32), precision=HIGHEST)


def reference(points, leaf_basis, right_sides, leaf_order, local_up, local_down, local_links, upper_nodes):
    floats = jnp.float32
    offsets = (jnp.arange(NPTS, dtype=jnp.int32) // PTS_DEV) * PTS_DEV
    sources = (offsets + leaf_order).astype(jnp.int32)
    gathered = jnp.take(right_sides, sources, axis=1)
    device_rhs = gathered.reshape(COLS, DEVICES, PTS_DEV).transpose(1, 0, 2)
    device_basis = leaf_basis.reshape(DEVICES, PTS_DEV, RANK)
    device_points = points.reshape(DIMS, DEVICES, PTS_DEV).transpose(1, 0, 2)

    def leaf_up(operands):
        block_rhs, block_basis = operands
        shaped_rhs = block_rhs.reshape(COLS, LEAVES_DEV, LEAF).astype(floats)
        shaped_basis = block_basis.reshape(LEAVES_DEV, LEAF, RANK).astype(floats)
        return jnp.einsum('kal,alr->akr', shaped_rhs, shaped_basis, precision=HIGHEST)

    coefficients = [lax.map(leaf_up, (device_rhs, device_basis)).reshape(ALL_LEAVES, COLS, RANK)]

    up_device = local_up.reshape(DEVICES, 2 * LEAVES_DEV - 2, RANK, RANK)
    down_device = local_down.reshape(DEVICES, 2 * LEAVES_DEV - 2, RANK, RANK)
    link_device = local_links.reshape(DEVICES, LEAVES_DEV - 1, 2, RANK, RANK)
    lift_mats = []
    lower_mats = []
    couple_mats = []
    for height in range(LOCAL_LEVELS):
        number = LEAVES_DEV >> height
        offset = 2 * LEAVES_DEV - 2 * number
        first = LEAVES_DEV - number
        lift_mats.append(up_device[:, offset:offset + number].reshape(DEVICES * number, RANK, RANK))
        lower_mats.append(down_device[:, offset:offset + number].reshape(DEVICES * number, RANK, RANK))
        couple_mats.append(link_device[:, first:first + number // 2].reshape(DEVICES * number, RANK, RANK))
    for tier in range(CROSS_LEVELS):
        chosen = upper_nodes[::2 ** tier, tier]
        lift_mats.append(chosen[:, 0])
        lower_mats.append(chosen[:, 1])
        couple_mats.append(chosen[:, 2])

    total_levels = LOCAL_LEVELS + CROSS_LEVELS
    for height in range(1, total_levels):
        moved = batched(coefficients[-1], lift_mats[height - 1])
        coefficients.append(moved.reshape(-1, 2, COLS, RANK).sum(axis=1))

    far_field = jnp.zeros((1, COLS, RANK), floats)
    for height in reversed(range(total_levels)):
        level_coef = coefficients[height]
        number = level_coef.shape[0]
        sibling = level_coef.reshape(number // 2, 2, COLS, RANK)[:, ::-1].reshape(number, COLS, RANK)
        parent = jnp.repeat(far_field, 2, axis=0)
        far_field = batched(parent, lower_mats[height]) + batched(sibling, couple_mats[height])

    device_far = far_field.reshape(DEVICES, LEAVES_DEV, COLS, RANK)

    def leaf_out(operands):
        block_points, block_rhs, block_basis, block_far = operands
        blocks = kernel_blocks(block_points.reshape(DIMS, LEAVES_DEV, LEAF)).astype(floats)
        shaped_rhs = block_rhs.reshape(COLS, LEAVES_DEV, LEAF).astype(floats)
        near_part = jnp.einsum('kal,alm->kam', shaped_rhs, blocks, precision=HIGHEST)
        shaped_basis = block_basis.reshape(LEAVES_DEV, LEAF, RANK).astype(floats)
        far_part = jnp.einsum('akr,alr->kal', rounded(block_far), shaped_basis, precision=HIGHEST)
        return (near_part + far_part).reshape(COLS, PTS_DEV)

    outputs = lax.map(leaf_out, (device_points, device_rhs, device_basis, device_far))
    outputs = outputs.transpose(1, 0, 2).reshape(COLS, NPTS)
    return jnp.zeros((COLS, NPTS), floats).at[:, sources].set(outputs)
```

```python
import math

import jax
import jax.numpy as jnp
from jax import lax
from jax.experimental import pallas as pl
from jax.experimental.pallas import tpu as pltpu
from jax.sharding import PartitionSpec as P

MESH = pl.DeviceIdType.MESH
F32 = jnp.float32
BF16 = jnp.bfloat16
LEAVES = 8
LEAF = 512
RANK = 256
COLS = 32
PTS = 4096
DIMS = 64
LOW = 256
HIGH = PTS // LOW
SCALE = math.sqrt(math.log2(math.e) * 4.0 / DIMS)


def flip(value, mask):
    for bit in (1, 2, 4):
        if mask & bit:
            value = value + bit * (1 - 2 * ((value // bit) % 2))
    return value


def halves(values):
    top = values.astype(BF16)
    rest = (values - top.astype(F32)).astype(BF16)
    return jnp.concatenate([top, rest], axis=0)


def times(values, matrix):
    rows = values.shape[0]
    both = jnp.dot(halves(values), matrix, preferred_element_type=F32)
    return both[:rows] + both[rows:]


def kernel(
    points_h, basis_h, rhs_h, order_h, up_h, down_h, links_h, upper_h,
    out_h,
    points_v, basis_v, rhs_v, order_v, up_v, down_v, links_v, upper_v,
    stack_v, hot_v, x_v, near_v, acc_v, out_v,
    xh0, xh1, xh2, cpl, root_v, sib0, lift1, lift1_in,
    s1_v, l2_v, l3_v, y_in, yq_in, far_v, e_v,
    x_out, x_in, z_out, z_in, y3_v,
    load_sem, store_sem, send_sem, recv_sem,
):
    z = lax.axis_index("leaf")
    w = lax.axis_index("wide")
    c = w % 2
    y = (w // 2) % 4
    x = w // 8

    def device(dz=0, dx=0, dy=0, dc=0):
        return (flip(z, dz), flip(x, dx) * 8 + flip(y, dy) * 2 + flip(c, dc))

    peers = [dict(dc=1)]
    peers += [dict(dy=m) for m in (1, 2, 3)]
    peers += [dict(dy=m, dc=1) for m in (1, 2, 3)]
    peers += [dict(dx=m) for m in (1, 2, 3)]
    peers += [dict(dz=m) for m in range(1, 8)]

    pairs = [
        (order_h, order_v), (rhs_h, rhs_v), (basis_h, basis_v), (up_h, up_v),
        (upper_h, upper_v), (points_h, points_v), (links_h, links_v), (down_h, down_v),
    ]
    loads = [
        pltpu.make_async_copy(src, dst, load_sem.at[i])
        for i, (src, dst) in enumerate(pairs)
    ]
    for load in loads:
        load.start()
    ld_order, ld_rhs, ld_basis, ld_up, ld_upper, ld_points, ld_links, ld_down = loads

    barrier = pltpu.get_barrier_semaphore()
    for peer in peers:
        pl.semaphore_signal(barrier, inc=1, device_id=device(**peer), device_id_type=MESH)

    sends = []

    def send(src, dst, slot, peer):
        copy = pltpu.make_async_remote_copy(
            src_ref=src,
            dst_ref=dst,
            send_sem=send_sem.at[slot],
            recv_sem=recv_sem.at[slot],
            device_id=device(**peer),
            device_id_type=MESH,
        )
        copy.start()
        sends.append(copy)
        return copy

    def order_row(a):
        rows = order_v[pl.ds(a * 4, 4), :]
        return jnp.concatenate([rows[i : i + 1] for i in range(4)], axis=1)

    ld_order.wait()
    ld_rhs.wait()
    for h in range(HIGH):
        stack_v[h * COLS : (h + 1) * COLS, :] = rhs_v[:, h * LOW : (h + 1) * LOW]
    ld_basis.wait()

    def leaf_up(a, carry):
        cols = pl.ds(pl.multiple_of(a * LEAF, LEAF), LEAF)
        row = order_row(a)
        low = row % LOW
        high = row // LOW
        place = lax.broadcasted_iota(jnp.int32, (LOW, LEAF), 0)
        hot = jnp.where(place == low, 1.0, 0.0).astype(BF16)
        hot_v[:, cols] = hot
        every = jnp.dot(stack_v[...], hot, preferred_element_type=F32)
        found = every[:COLS]
        for h in range(1, HIGH):
            found = jnp.where(high == h, every[h * COLS : (h + 1) * COLS], found)
        found = found.astype(BF16)
        x_v[:, cols] = found
        xh0[a] = jnp.dot(found, basis_v[cols, :], preferred_element_type=F32)
        return carry

    lax.fori_loop(0, LEAVES, leaf_up, 0)

    def lift_pair(ref, n, first):
        both = jnp.concatenate([ref[2 * n], ref[2 * n + 1]], axis=1)
        mats = up_v[first + 2 * n : first + 2 * n + 2].reshape(2 * RANK, RANK)
        return times(both, mats)

    ld_up.wait()
    for n in range(4):
        xh1[n] = lift_pair(xh0, n, 0)
    for n in range(2):
        xh2[n] = lift_pair(xh1, n, 8)
    root = lift_pair(xh2, 0, 12)
    root_v[...] = root

    pl.semaphore_wait(barrier, len(peers))
    core = dict(dc=1)
    got_sib0 = send(root_v, sib0, 0, core)
    ld_upper.wait()
    lift = times(root, upper_v[0, 0])
    lift1[0] = lift[:16]
    lift1[1] = lift[16:]
    got_lift1 = send(lift1.at[1 - c], lift1_in, 1, core)

    def near(a, carry):
        cols = pl.ds(pl.multiple_of(a * LEAF, LEAF), LEAF)
        p = points_v[:, cols] * SCALE
        top = p.astype(BF16)
        rest = (p - top.astype(F32)).astype(BF16)
        norm = -0.5 * jnp.sum(p * p, axis=0, keepdims=True)
        n1 = norm.astype(BF16).astype(F32)
        n2 = (norm - n1).astype(BF16).astype(F32)
        n3 = norm - n1 - n2
        row = lax.broadcasted_iota(jnp.int32, (16, LEAF), 0)
        one = jnp.where(row < 6, 1.0, 0.0)
        left = jnp.where(row == 0, n1, jnp.where(row == 1, n2, jnp.where(row == 2, n3, one)))
        right = jnp.where(row == 3, n1, jnp.where(row == 4, n2, jnp.where(row == 5, n3, one)))
        pad = jnp.zeros((48, LEAF), BF16)
        a1 = jnp.concatenate([top, rest, top, left.astype(BF16), pad], axis=0)
        a2 = jnp.concatenate([top, top, rest, right.astype(BF16), pad], axis=0)
        power = lax.dot_general(a1, a2, (((0,), (0,)), ((), ())), preferred_element_type=F32)
        block = jnp.exp2(power).astype(BF16)
        rhs = x_v[:, cols]
        near_v[:, cols] = jnp.dot(rhs, block, preferred_element_type=F32) + rhs.astype(F32)
        return carry

    ld_points.wait()
    lax.fori_loop(0, 2, near, 0)

    got_lift1.wait_recv()
    s1 = lift1[c] + lift1_in[...]
    s1_v[...] = s1

    l2 = times(s1, upper_v[1, 0])
    l3 = times(l2, upper_v[2, 0])
    l2_v[...] = l2
    for q in range(4):
        l3_v[q] = l3[q * 4 : q * 4 + 4]
    got_y = []
    got_yq = []
    for m in (1, 2, 3):
        got_y.append(send(s1_v if m == 1 else l2_v, y_in.at[m - 1], 1 + m, dict(dy=m)))
        got_yq.append(send(l3_v.at[flip(y, m)], yq_in.at[m - 1], 4 + m, dict(dy=m)))

    lax.fori_loop(2, 4, near, 0)

    for copy in got_yq:
        copy.wait_recv()
    s3 = (l3_v[y] + yq_in[0]) + (yq_in[1] + yq_in[2])
    l4 = times(s3, upper_v[3, 0])
    l5 = times(l4, upper_v[4, 0])
    x_out[0, 0] = s3
    x_out[0, 1] = l5
    x_out[1, 0] = l4
    x_out[1, 1] = l5
    got_x = []
    for m in (1, 2, 3):
        got_x.append(send(x_out.at[0 if m == 1 else 1], x_in.at[m - 1], 7 + m, dict(dx=m)))

    for copy in got_y:
        copy.wait_recv()
    e = times(times(y_in[1] + y_in[2], upper_v[2, 2]), upper_v[1, 1])
    e = e + times(y_in[0], upper_v[1, 2])
    e_v[c] = e
    got_e = send(e_v.at[c], e_v.at[c], 11, core)

    lax.fori_loop(4, 6, near, 0)

    for copy in got_x:
        copy.wait_recv()
    s5 = (l5 + x_in[0, 1]) + (x_in[1, 1] + x_in[2, 1])
    l6 = times(s5, upper_v[5, 0])
    l7 = times(l6, upper_v[6, 0])
    z_out[0] = s5
    z_out[1] = l6
    z_out[2] = l7
    got_z = []
    for m in range(1, 8):
        src = z_out.at[m.bit_length() - 1]
        got_z.append(send(src, z_in.at[m - 1], 11 + m, dict(dz=m)))

    c3 = times(x_in[0, 0], upper_v[3, 2])
    c4 = times(x_in[1, 0] + x_in[2, 0], upper_v[4, 2])

    ld_links.wait()
    for m in range(8):
        cpl[m] = times(xh0[m ^ 1], links_v[m // 2, m % 2])
    for m in range(4):
        cpl[8 + m] = times(xh1[m ^ 1], links_v[4 + m // 2, m % 2])
    for m in range(2):
        cpl[12 + m] = times(xh2[m ^ 1], links_v[6, m])
    got_sib0.wait_recv()
    c0 = times(sib0[...], upper_v[0, 2])
    got_e.wait_recv()
    c0 = c0 + times(e_v[...].reshape(COLS, RANK), upper_v[0, 1])

    lax.fori_loop(6, 8, near, 0)

    for copy in got_z:
        copy.wait_recv()
    sib5 = z_in[0]
    sib6 = z_in[1] + z_in[2]
    sib7 = (z_in[3] + z_in[4]) + (z_in[5] + z_in[6])
    c5 = times(sib5, upper_v[5, 2])
    c6 = times(sib6, upper_v[6, 2])
    y7 = times(sib7, upper_v[7, 2])
    y6 = times(y7, upper_v[6, 1]) + c6
    y5 = times(y6, upper_v[5, 1]) + c5
    y4 = times(y5, upper_v[4, 1]) + c4
    y3 = times(y4, upper_v[3, 1]) + c3
    slot = c * 4 + y
    y3_v[slot] = y3
    got_y3 = []
    for i, peer in enumerate(peers[:7]):
        got_y3.append(send(y3_v.at[slot], y3_v.at[slot], 19 + i, peer))
    ld_down.wait()
    for copy in got_y3:
        copy.wait_recv()
    y3 = jnp.concatenate([y3_v[i] for i in range(8)], axis=0)
    y2 = times(y3, upper_v[2, 1])
    y1 = times(y2, upper_v[1, 1])
    current = [times(y1, upper_v[0, 1]) + c0]
    for number, first in ((2, 12), (4, 8), (8, 0)):
        current = [
            times(current[m // 2], down_v[first + m]) + cpl[first + m] for m in range(number)
        ]
    for m in range(8):
        far_v[m] = current[m].astype(BF16)

    acc_v[...] = jnp.zeros_like(acc_v)

    def leaf_out(a, carry):
        cols = pl.ds(pl.multiple_of(a * LEAF, LEAF), LEAF)
        far = lax.dot_general(
            far_v[a], basis_v[cols, :], (((1,), (1,)), ((), ())), preferred_element_type=F32
        )
        total = near_v[:, cols] + far
        high = order_row(a) // LOW
        top = total.astype(BF16)
        rest = (total - top.astype(F32)).astype(BF16)
        tops, rests = [], []
        for h in range(HIGH):
            mask = jnp.where(high == h, 1.0, 0.0).astype(BF16)
            tops.append(top * mask)
            rests.append(rest * mask)
        hot = hot_v[:, cols]
        nt = (((1,), (1,)), ((), ()))
        wide = jnp.concatenate(tops, axis=0)
        slim = jnp.concatenate(rests, axis=0)
        acc_v[...] += lax.dot_general(wide, hot, nt, preferred_element_type=F32) + lax.dot_general(
            slim, hot, nt, preferred_element_type=F32
        )
        return carry

    lax.fori_loop(0, LEAVES, leaf_out, 0)
    for h in range(HIGH):
        out_v[:, h * LOW : (h + 1) * LOW] = acc_v[h * COLS : (h + 1) * COLS, :]
    store = pltpu.make_async_copy(out_v, out_h, store_sem)
    store.start()
    for copy in sends:
        copy.wait_send()
    store.wait()


def on_device(
    points, leaf_basis, right_sides, leaf_order, local_up, local_down, local_links, upper_nodes
):
    vm = pltpu.VMEM
    scratch = [
        vm((DIMS, PTS), F32),
        vm((PTS, RANK), BF16),
        vm((COLS, PTS), BF16),
        vm((32, 128), jnp.int32),
        vm((14, RANK, RANK), BF16),
        vm((14, RANK, RANK), BF16),
        vm((7, 2, RANK, RANK), BF16),
        vm((8, 3, RANK, RANK), BF16),
        vm((HIGH * COLS, LOW), BF16),
        vm((LOW, PTS), BF16),
        vm((COLS, PTS), BF16),
        vm((COLS, PTS), F32),
        vm((HIGH * COLS, LOW), F32),
        vm((COLS, PTS), F32),
        vm((8, COLS, RANK), F32),
        vm((4, COLS, RANK), F32),
        vm((2, COLS, RANK), F32),
        vm((14, COLS, RANK), F32),
        vm((COLS, RANK), F32),
        vm((COLS, RANK), F32),
        vm((2, 16, RANK), F32),
        vm((16, RANK), F32),
        vm((16, RANK), F32),
        vm((16, RANK), F32),
        vm((4, 4, RANK), F32),
        vm((3, 16, RANK), F32),
        vm((3, 4, RANK), F32),
        vm((8, COLS, RANK), BF16),
        vm((2, 16, RANK), F32),
        vm((2, 2, 4, RANK), F32),
        vm((3, 2, 4, RANK), F32),
        vm((3, 4, RANK), F32),
        vm((7, 4, RANK), F32),
        vm((8, 4, RANK), F32),
        pltpu.SemaphoreType.DMA((8,)),
        pltpu.SemaphoreType.DMA,
        pltpu.SemaphoreType.DMA((26,)),
        pltpu.SemaphoreType.DMA((26,)),
    ]
    return pl.pallas_call(
        kernel,
        out_shape=jax.ShapeDtypeStruct((COLS, PTS), F32),
        in_specs=[pl.BlockSpec(memory_space=pl.ANY)] * 8,
        out_specs=pl.BlockSpec(memory_space=pl.ANY),
        scratch_shapes=scratch,
        compiler_params=pltpu.CompilerParams(
            collective_id=0, has_side_effects=True, vmem_limit_bytes=56 * 2**20
        ),
    )(
        points, leaf_basis, right_sides, leaf_order.reshape(32, 128), local_up, local_down,
        local_links, upper_nodes.reshape(8, 3, RANK, RANK),
    )


def solution(mesh):
    in_specs = (
        P(None, ("leaf", "wide")),
        P(("leaf", "wide"), None),
        P(None, ("leaf", "wide")),
        P(("leaf", "wide")),
        P(("leaf", "wide"), None, None),
        P(("leaf", "wide"), None, None),
        P(("leaf", "wide"), None, None, None),
        P(("leaf", "wide"), None, None, None, None),
    )
    out_specs = P(None, ("leaf", "wide"))
    return jax.shard_map(
        on_device, mesh=mesh, in_specs=in_specs, out_specs=out_specs, check_vma=False
    )
```

```python
import math

import jax
import jax.numpy as jnp
from jax import lax
from jax.experimental import pallas as pl
from jax.experimental.pallas import tpu as pltpu
from jax.sharding import PartitionSpec as P

MESH = pl.DeviceIdType.MESH
F32 = jnp.float32
BF16 = jnp.bfloat16
LEAVES = 8
LEAF = 512
RANK = 256
COLS = 32
PTS = 4096
DIMS = 64
LOW = 256
HIGH = PTS // LOW
UP_UNROLL = 1
SCALE = math.sqrt(math.log2(math.e) * 4.0 / DIMS)


def flip(value, mask):
    for bit in (1, 2, 4):
        if mask & bit:
            value = value + bit * (1 - 2 * ((value // bit) % 2))
    return value


def halves(values):
    top = values.astype(BF16)
    rest = (values - top.astype(F32)).astype(BF16)
    return jnp.concatenate([top, rest], axis=0)


def times(values, matrix):
    rows = values.shape[0]
    both = jnp.dot(halves(values), matrix, preferred_element_type=F32)
    return both[:rows] + both[rows:]


def pair(values):
    top = values.astype(BF16)
    return top, (values - top.astype(F32)).astype(BF16)


def times_pair(values, top, rest):
    rows = values.shape[0]
    parts = halves(values)
    both = jnp.dot(parts, top, preferred_element_type=F32)
    return both[:rows] + both[rows:] + jnp.dot(parts[:rows], rest, preferred_element_type=F32)


PLANE = sorted(
    (
        dict(dx=dx, dy=dy, dc=dc)
        for dx in range(4)
        for dy in range(4)
        for dc in range(2)
        if dx or dy or dc
    ),
    key=lambda p: -(p["dx"] > 0) - (p["dx"] == 2) - (p["dy"] > 0) - (p["dy"] == 2),
)
FAR_Z = (4, 3, 5, 2, 6, 7, 1)


def kernel(
    points_h, basis_h, rhs_h, order_h, up_h, down_h, links_h, upper_h,
    out_h,
    points_v, basis_v, rhs_v, order_v, up_v, down_v, links_v, p_v, qb_v,
    stack_v, hot_v, x_v, acc_v, out_v,
    xh0, xh1, xh2, cpl, root_v, sib0, half_v, quart_v, plane_in, low_in, y_in,
    e_v, z_out, z_in, y3_v, m_top, m_rest, w_top, w_rest, w1_v, g_v,
    load_sem, store_sem, one_send, one_recv, plane_send, plane_recv, low_send, low_recv,
):
    z = lax.axis_index("leaf")
    w = lax.axis_index("wide")
    c = w % 2
    y = (w // 2) % 4
    x = w // 8

    def device(dz=0, dx=0, dy=0, dc=0):
        return (flip(z, dz), flip(x, dx) * 8 + flip(y, dy) * 2 + flip(c, dc))

    def quarter(dx=0, dy=0, dc=0):
        return flip(c, dc) * 4 + flip(y, dy)

    def load(i, src, dst):
        copy = pltpu.make_async_copy(src, dst, load_sem.at[i])
        copy.start()
        return copy

    ld_order = load(0, order_h, order_v)
    ld_rhs = load(1, rhs_h, rhs_v)
    ld_basis = load(2, basis_h, basis_v)
    ld_up = load(3, up_h, up_v)
    ld_p = load(4, upper_h.at[:, 0], p_v)

    barrier = pltpu.get_barrier_semaphore()
    peers = PLANE + [dict(dz=m) for m in FAR_Z]
    for peer in peers:
        pl.semaphore_signal(barrier, inc=1, device_id=device(**peer), device_id_type=MESH)

    sends = []

    def send(src, dst, send_sem, recv_sem, peer):
        copy = pltpu.make_async_remote_copy(
            src_ref=src,
            dst_ref=dst,
            send_sem=send_sem,
            recv_sem=recv_sem,
            device_id=device(**peer),
            device_id_type=MESH,
        )
        copy.start()
        return copy

    def send_one(src, dst, slot, peer):
        copy = send(src, dst, one_send.at[slot], one_recv.at[slot], peer)
        sends.append(copy)
        return copy

    def order_row(a):
        rows = order_v[pl.ds(a * 4, 4), :]
        return jnp.concatenate([rows[i : i + 1] for i in range(4)], axis=1)

    def leaf_cols(a):
        return pl.ds(pl.multiple_of(a * LEAF, LEAF), LEAF)

    ld_order.wait()
    ld_rhs.wait()
    for h in range(HIGH):
        stack_v[h * COLS : (h + 1) * COLS, :] = rhs_v[:, h * LOW : (h + 1) * LOW]
    ld_basis.wait()
    ld_points = load(5, points_h, points_v)
    ld_links = load(6, links_h, links_v)
    ld_down = load(7, down_h, down_v)
    ld_qb = load(8, upper_h.at[:, 1:], qb_v)

    def leaf_up(a):
        cols = leaf_cols(a)
        row = order_row(a)
        low = row % LOW
        high = row // LOW
        place = lax.broadcasted_iota(jnp.int32, (LOW, LEAF), 0)
        hot = jnp.where(place == low, 1.0, 0.0).astype(BF16)
        hot_v[:, cols] = hot
        every = jnp.dot(stack_v[...], hot, preferred_element_type=F32)
        found = every[:COLS]
        for h in range(1, HIGH):
            found = jnp.where(high == h, every[h * COLS : (h + 1) * COLS], found)
        found = found.astype(BF16)
        x_v[:, cols] = found
        xh0[a] = jnp.dot(found, basis_v[cols, :], preferred_element_type=F32)

    def leaf_ups(i, carry):
        for j in range(UP_UNROLL):
            leaf_up(i * UP_UNROLL + j)
        return carry

    lax.fori_loop(0, LEAVES // UP_UNROLL, leaf_ups, 0)

    def lift_pair(ref, n, first):
        both = jnp.concatenate([ref[2 * n], ref[2 * n + 1]], axis=1)
        mats = up_v[first + 2 * n : first + 2 * n + 2].reshape(2 * RANK, RANK)
        return times(both, mats)

    ld_up.wait()
    for n in range(4):
        xh1[n] = lift_pair(xh0, n, 0)
    for n in range(2):
        xh2[n] = lift_pair(xh1, n, 8)
    root = lift_pair(xh2, 0, 12)

    ld_p.wait()
    lift = [root]
    for level in range(5):
        lift.append(times(lift[-1], p_v[level]))
    for q in range(8):
        quart_v[2, q] = lift[5][q * 4 : q * 4 + 4]
    pl.semaphore_wait(barrier, len(peers))
    for i, peer in enumerate(PLANE):
        send(quart_v.at[2, quarter(**peer)], plane_in.at[i], plane_send, plane_recv, peer)
    root_v[...] = root
    core = dict(dc=1)
    got_sib0 = send_one(root_v, sib0, 0, core)
    for level in (1, 2):
        for half in range(2):
            half_v[level - 1, half] = lift[level][half * 16 : half * 16 + 16]
    for level in (3, 4):
        for q in range(8):
            quart_v[level - 3, q] = lift[level][q * 4 : q * 4 + 4]

    def scatter(a, parts):
        high = jnp.broadcast_to(order_row(a) // LOW, (16, LEAF))
        rows = []
        for h in range(HIGH):
            mask = jnp.where(high == h, 1.0, 0.0).astype(BF16)
            mask = jnp.concatenate([mask, mask], axis=0)
            rows += [part * mask for part in parts]
        rows = jnp.concatenate(rows, axis=0)
        return lax.dot_general(
            rows, hot_v[:, leaf_cols(a)], (((1,), (1,)), ((), ())), preferred_element_type=F32
        )

    def near(a, carry):
        cols = leaf_cols(a)
        p = points_v[:, cols] * SCALE
        top, rest = pair(p)
        norm = -0.5 * jnp.sum(p * p, axis=0, keepdims=True)
        n1 = norm.astype(BF16).astype(F32)
        n2 = (norm - n1).astype(BF16).astype(F32)
        n3 = norm - n1 - n2
        row = lax.broadcasted_iota(jnp.int32, (16, LEAF), 0)
        one = jnp.where(row < 6, 1.0, 0.0)
        left = jnp.where(row == 0, n1, jnp.where(row == 1, n2, jnp.where(row == 2, n3, one)))
        right = jnp.where(row == 3, n1, jnp.where(row == 4, n2, jnp.where(row == 5, n3, one)))
        pad = jnp.zeros((48, LEAF), BF16)
        a1 = jnp.concatenate([top, rest, top, left.astype(BF16), pad], axis=0)
        a2 = jnp.concatenate([top, top, rest, right.astype(BF16), pad], axis=0)
        power = lax.dot_general(a1, a2, (((0,), (0,)), ((), ())), preferred_element_type=F32)
        block = jnp.exp2(power).astype(BF16)
        rhs = x_v[:, cols]
        total = jnp.dot(rhs, block, preferred_element_type=F32) + rhs.astype(F32)
        both = scatter(a, pair(total))
        for h in range(HIGH):
            at = 2 * h * COLS
            acc_v[h * COLS : (h + 1) * COLS, :] += both[at : at + COLS] + both[at + COLS : at + 2 * COLS]
        return carry

    ld_points.wait()
    acc_v[...] = jnp.zeros_like(acc_v)
    lax.fori_loop(0, 1, near, 0)

    got_y = []
    for i in range(6):
        m = 3 - i // 2
        peer = dict(dy=m, dc=i % 2)
        src = half_v.at[0 if m == 1 else 1, flip(c, i % 2)]
        got_y.append(send_one(src, y_in.at[i], 1 + i, peer))
    lower = [peer for peer in PLANE if peer["dx"]]
    for i, peer in enumerate(lower):
        src = quart_v.at[0 if peer["dx"] == 1 else 1, quarter(**peer)]
        send(src, low_in.at[i], low_send, low_recv, peer)

    lax.fori_loop(1, 6, near, 0)

    pltpu.make_async_copy(plane_in, plane_in, plane_recv).wait()
    s5 = jnp.sum(plane_in[...], axis=0) + quart_v[2, quarter()]
    l6 = times(s5, p_v[5])
    l7 = times(l6, p_v[6])
    z_out[0] = s5
    z_out[1] = l6
    z_out[2] = l7
    got_z = []
    for m in FAR_Z:
        got_z.append(send_one(z_out.at[m.bit_length() - 1], z_in.at[m - 1], 7 + m, dict(dz=m)))

    ld_qb.wait()

    def q_of(level):
        return qb_v[level, 0]

    def b_of(level):
        return qb_v[level, 1]

    m7 = jnp.dot(b_of(7), q_of(6), preferred_element_type=F32)
    both = jnp.dot(
        jnp.concatenate([halves(m7), b_of(6)], axis=0), q_of(5), preferred_element_type=F32
    )
    m7 = both[:RANK] + both[RANK : 2 * RANK]
    m6 = both[2 * RANK :]
    both = jnp.dot(
        jnp.concatenate([halves(m7), halves(m6), b_of(5)], axis=0), q_of(4), preferred_element_type=F32
    )
    m7 = both[:RANK] + both[RANK : 2 * RANK]
    m6 = both[2 * RANK : 3 * RANK] + both[3 * RANK : 4 * RANK]
    m5 = both[4 * RANK :]
    for i, mat in enumerate((m7, m6, m5)):
        mat = times(mat, q_of(3))
        m_top[i * RANK : (i + 1) * RANK], m_rest[i * RANK : (i + 1) * RANK] = pair(mat)

    ld_links.wait()
    for m in range(8):
        cpl[m] = times(xh0[m ^ 1], links_v[m // 2, m % 2])
    for m in range(4):
        cpl[8 + m] = times(xh1[m ^ 1], links_v[4 + m // 2, m % 2])
    for m in range(2):
        cpl[12 + m] = times(xh2[m ^ 1], links_v[6, m])

    for copy in got_y:
        copy.wait_recv()
    sib2 = (y_in[0] + y_in[1]) + (y_in[2] + y_in[3])
    sib1 = y_in[4] + y_in[5]
    e = times(times(sib2, b_of(2)), q_of(1)) + times(sib1, b_of(1))
    e_v[c] = e
    got_e = send_one(e_v.at[c], e_v.at[c], 15, core)

    pltpu.make_async_copy(low_in, low_in, low_recv).wait()
    sib3 = jnp.zeros((4, RANK), F32)
    sib4 = jnp.zeros((4, RANK), F32)
    for i, peer in enumerate(lower):
        if peer["dx"] == 1:
            sib3 = sib3 + low_in[i]
        else:
            sib4 = sib4 + low_in[i]
    c34 = times(times(sib4, b_of(4)), q_of(3)) + times(sib3, b_of(3))

    ld_down.wait()
    t = times(times(jnp.dot(q_of(2), q_of(1), preferred_element_type=F32), q_of(0)), down_v[12])
    w1_v[0] = t
    t = times(times(jnp.dot(q_of(2), q_of(1), preferred_element_type=F32), q_of(0)), down_v[13])
    w1_v[1] = t

    def chain_1(m, carry):
        w1_v[2 + m] = times(w1_v[m // 2], down_v[8 + m])
        return carry

    def chain_0(m, carry):
        top, rest = pair(times(w1_v[2 + m // 2], down_v[m]))
        w_top[m] = top
        w_rest[m] = rest
        return carry

    lax.fori_loop(0, 4, chain_1, 0)
    lax.fori_loop(0, 8, chain_0, 0)

    for copy in got_z:
        copy.wait_recv()
    sib5 = z_in[0]
    sib6 = z_in[1] + z_in[2]
    sib7 = (z_in[3] + z_in[4]) + (z_in[5] + z_in[6])
    y3 = times_pair(jnp.concatenate([sib7, sib6, sib5], axis=1), m_top[...], m_rest[...]) + c34
    mine = quarter()
    y3_v[mine] = y3
    got_y3 = []
    for i, peer in enumerate([p for p in PLANE if p["dx"] == 0]):
        got_y3.append(send_one(y3_v.at[mine], y3_v.at[mine], 16 + i, peer))

    got_sib0.wait_recv()
    got_e.wait_recv()
    current = [times(sib0[...], b_of(0)) + times(e_v[...].reshape(COLS, RANK), q_of(0))]
    for number, first in ((2, 12), (4, 8), (8, 0)):
        current = [
            times(current[m // 2], down_v[first + m]) + cpl[first + m] for m in range(number)
        ]
    for m in range(8):
        g_v[m] = current[m]
    lax.fori_loop(6, 8, near, 0)
    pltpu.make_async_copy(plane_in, plane_in, plane_send).wait()
    pltpu.make_async_copy(low_in, low_in, low_send).wait()
    for copy in sends[:-7]:
        copy.wait_send()

    for copy in got_y3:
        copy.wait_recv()
    y3 = jnp.concatenate([y3_v[i] for i in range(8)], axis=0)

    def leaf_out(a):
        far = (times_pair(y3, w_top[a], w_rest[a]) + g_v[a]).astype(BF16)
        far = lax.dot_general(
            far, basis_v[leaf_cols(a), :], (((1,), (1,)), ((), ())), preferred_element_type=F32
        )
        return scatter(a, (far.astype(BF16),))

    def leaf_outs(i, carry):
        total = leaf_out(2 * i) + leaf_out(2 * i + 1)
        acc_v[...] += total
        return carry

    lax.fori_loop(0, LEAVES // 2, leaf_outs, 0)
    for h in range(HIGH):
        out_v[:, h * LOW : (h + 1) * LOW] = acc_v[h * COLS : (h + 1) * COLS, :]
    store = pltpu.make_async_copy(out_v, out_h, store_sem)
    store.start()
    for copy in sends[-7:]:
        copy.wait_send()
    store.wait()


def on_device(
    points, leaf_basis, right_sides, leaf_order, local_up, local_down, local_links, upper_nodes
):
    vm = pltpu.VMEM
    dma = pltpu.SemaphoreType.DMA
    scratch = [
        vm((DIMS, PTS), F32),
        vm((PTS, RANK), BF16),
        vm((COLS, PTS), BF16),
        vm((32, 128), jnp.int32),
        vm((14, RANK, RANK), BF16),
        vm((14, RANK, RANK), BF16),
        vm((7, 2, RANK, RANK), BF16),
        vm((8, RANK, RANK), BF16),
        vm((8, 2, RANK, RANK), BF16),
        vm((HIGH * COLS, LOW), BF16),
        vm((LOW, PTS), BF16),
        vm((COLS, PTS), BF16),
        vm((HIGH * COLS, LOW), F32),
        vm((COLS, PTS), F32),
        vm((8, COLS, RANK), F32),
        vm((4, COLS, RANK), F32),
        vm((2, COLS, RANK), F32),
        vm((14, COLS, RANK), F32),
        vm((COLS, RANK), F32),
        vm((COLS, RANK), F32),
        vm((2, 2, 16, RANK), F32),
        vm((3, 8, 4, RANK), F32),
        vm((31, 4, RANK), F32),
        vm((24, 4, RANK), F32),
        vm((6, 16, RANK), F32),
        vm((2, 16, RANK), F32),
        vm((3, 4, RANK), F32),
        vm((7, 4, RANK), F32),
        vm((8, 4, RANK), F32),
        vm((3 * RANK, RANK), BF16),
        vm((3 * RANK, RANK), BF16),
        vm((8, RANK, RANK), BF16),
        vm((8, RANK, RANK), BF16),
        vm((6, RANK, RANK), F32),
        vm((8, COLS, RANK), F32),
        dma((9,)),
        dma,
        dma((23,)),
        dma((23,)),
        dma,
        dma,
        dma,
        dma,
    ]
    return pl.pallas_call(
        kernel,
        out_shape=jax.ShapeDtypeStruct((COLS, PTS), F32),
        in_specs=[pl.BlockSpec(memory_space=pl.ANY)] * 8,
        out_specs=pl.BlockSpec(memory_space=pl.ANY),
        scratch_shapes=scratch,
        compiler_params=pltpu.CompilerParams(
            collective_id=0, has_side_effects=True, vmem_limit_bytes=56 * 2**20
        ),
    )(
        points, leaf_basis, right_sides, leaf_order.reshape(32, 128), local_up, local_down,
        local_links, upper_nodes.reshape(8, 3, RANK, RANK),
    )


def solution(mesh):
    in_specs = (
        P(None, ("leaf", "wide")),
        P(("leaf", "wide"), None),
        P(None, ("leaf", "wide")),
        P(("leaf", "wide")),
        P(("leaf", "wide"), None, None),
        P(("leaf", "wide"), None, None),
        P(("leaf", "wide"), None, None, None),
        P(("leaf", "wide"), None, None, None, None),
    )
    out_specs = P(None, ("leaf", "wide"))
    return jax.shard_map(
        on_device, mesh=mesh, in_specs=in_specs, out_specs=out_specs, check_vma=False
    )
```

```python
import math

import jax
import jax.numpy as jnp
from jax import lax
from jax.experimental import pallas as pl
from jax.experimental.pallas import tpu as pltpu
from jax.sharding import PartitionSpec as P

MESH = pl.DeviceIdType.MESH
F32 = jnp.float32
BF16 = jnp.bfloat16
LEAVES = 8
LEAF = 512
RANK = 256
COLS = 32
PTS = 4096
DIMS = 64
LOW = 256
HIGH = PTS // LOW
SCALE = math.sqrt(math.log2(math.e) * 4.0 / DIMS)


def flip(value, mask):
    for bit in (1, 2, 4):
        if mask & bit:
            value = value + bit * (1 - 2 * ((value // bit) % 2))
    return value


def halves(values):
    top = values.astype(BF16)
    rest = (values - top.astype(F32)).astype(BF16)
    return jnp.concatenate([top, rest], axis=0)


def times(values, matrix):
    rows = values.shape[0]
    both = jnp.dot(halves(values), matrix, preferred_element_type=F32)
    return both[:rows] + both[rows:]


def pair(values):
    top = values.astype(BF16)
    return top, (values - top.astype(F32)).astype(BF16)


def times_pair(values, top, rest):
    rows = values.shape[0]
    parts = halves(values)
    both = jnp.dot(parts, top, preferred_element_type=F32)
    return both[:rows] + both[rows:] + jnp.dot(parts[:rows], rest, preferred_element_type=F32)


PLANE = sorted(
    (
        dict(dx=dx, dy=dy, dc=dc)
        for dx in range(4)
        for dy in range(4)
        for dc in range(2)
        if dx or dy or dc
    ),
    key=lambda p: -(p["dx"] > 0) - (p["dx"] == 2) - (p["dy"] > 0) - (p["dy"] == 2),
)
FAR_Z = (4, 3, 5, 2, 6, 7, 1)


def kernel(
    points_h, basis_h, rhs_h, order_h, up_h, down_h, links_h, upper_h,
    out_h,
    points_v, basis_v, rhs_v, order_v, up_v, down_v, links_v, p_v, qb_v,
    stack_v, hot_v, mask_v, zs_v, x_v,
    xh0, xh1, xh2, cpl, root_v, sib0, half_v, quart_v, plane_in, low_in, y_in,
    e_v, z_out, z_in, y3_v, m_top, m_rest, w_top, w_rest, w1_v, g_v,
    load_sem, one_send, one_recv, plane_send, plane_recv, low_send, low_recv,
):
    z = lax.axis_index("leaf")
    w = lax.axis_index("wide")
    c = w % 2
    y = (w // 2) % 4
    x = w // 8

    def device(dz=0, dx=0, dy=0, dc=0):
        return (flip(z, dz), flip(x, dx) * 8 + flip(y, dy) * 2 + flip(c, dc))

    def quarter(dx=0, dy=0, dc=0):
        return flip(c, dc) * 4 + flip(y, dy)

    def load(i, src, dst):
        copy = pltpu.make_async_copy(src, dst, load_sem.at[i])
        copy.start()
        return copy

    ld_order = load(0, order_h, order_v)
    ld_rhs = load(1, rhs_h, rhs_v)
    ld_basis = load(2, basis_h, basis_v)
    ld_up = load(3, up_h, up_v)
    ld_p = load(4, upper_h.at[:, 0], p_v)

    barrier = pltpu.get_barrier_semaphore()
    peers = PLANE + [dict(dz=m) for m in FAR_Z]
    for peer in peers:
        pl.semaphore_signal(barrier, inc=1, device_id=device(**peer), device_id_type=MESH)

    sends = []

    def send(src, dst, send_sem, recv_sem, peer):
        copy = pltpu.make_async_remote_copy(
            src_ref=src,
            dst_ref=dst,
            send_sem=send_sem,
            recv_sem=recv_sem,
            device_id=device(**peer),
            device_id_type=MESH,
        )
        copy.start()
        return copy

    def send_one(src, dst, slot, peer):
        copy = send(src, dst, one_send.at[slot], one_recv.at[slot], peer)
        sends.append(copy)
        return copy

    def order_row(a):
        rows = order_v[pl.ds(a * 4, 4), :]
        return jnp.concatenate([rows[i : i + 1] for i in range(4)], axis=1)

    def leaf_cols(a):
        return pl.ds(pl.multiple_of(a * LEAF, LEAF), LEAF)

    ld_order.wait()
    ld_rhs.wait()
    for h in range(HIGH):
        stack_v[h * COLS : (h + 1) * COLS, :] = rhs_v[:, h * LOW : (h + 1) * LOW]
    def gather(a):
        row = order_row(a)
        low = row % LOW
        high = jnp.broadcast_to(row // LOW, (8, LEAF))
        place = lax.broadcasted_iota(jnp.int32, (LOW, LEAF), 0)
        hot = jnp.where(place == low, 1.0, 0.0).astype(BF16)
        every = jnp.dot(stack_v[...], hot, preferred_element_type=F32)
        every = every.reshape(HIGH, COLS // 8, 8, LEAF)
        found = every[0]
        for h in range(1, HIGH):
            found = jnp.where((high == h)[None], every[h], found)
        x_v[:, leaf_cols(a)] = found.reshape(COLS, LEAF).astype(BF16)

    def gathers(i, carry):
        gather(2 * i)
        gather(2 * i + 1)
        return carry

    lax.fori_loop(0, LEAVES // 2, gathers, 0)
    ld_basis.wait()
    ld_points = load(5, points_h, points_v)
    ld_qb = load(8, upper_h.at[:, 1:], qb_v)
    ld_links = load(6, links_h, links_v)
    ld_down = load(7, down_h, down_v)
    for a in range(LEAVES):
        cols = slice(a * LEAF, (a + 1) * LEAF)
        xh0[a] = jnp.dot(x_v[:, cols], basis_v[cols, :], preferred_element_type=F32)

    def lift_pair(ref, n, first):
        both = jnp.concatenate([ref[2 * n], ref[2 * n + 1]], axis=1)
        mats = up_v[first + 2 * n : first + 2 * n + 2].reshape(2 * RANK, RANK)
        return times(both, mats)

    ld_up.wait()
    for n in range(4):
        xh1[n] = lift_pair(xh0, n, 0)
    for n in range(2):
        xh2[n] = lift_pair(xh1, n, 8)
    root = lift_pair(xh2, 0, 12)

    ld_p.wait()
    lift = [root]
    for level in range(5):
        lift.append(times(lift[-1], p_v[level]))
    for q in range(8):
        quart_v[2, q] = lift[5][q * 4 : q * 4 + 4]
    pl.semaphore_wait(barrier, len(peers))
    for i, peer in enumerate(PLANE):
        send(quart_v.at[2, quarter(**peer)], plane_in.at[i], plane_send, plane_recv, peer)
    root_v[...] = root
    core = dict(dc=1)
    got_sib0 = send_one(root_v, sib0, 0, core)
    for level in (1, 2):
        for half in range(2):
            half_v[level - 1, half] = lift[level][half * 16 : half * 16 + 16]
    for level in (3, 4):
        for q in range(8):
            quart_v[level - 3, q] = lift[level][q * 4 : q * 4 + 4]

    def spread(a, parts):
        rows = []
        for h in range(HIGH):
            mask = mask_v[h, :, leaf_cols(a)]
            mask = jnp.concatenate([mask, mask], axis=0)
            rows += [part * mask for part in parts]
        return jnp.concatenate(rows, axis=0)

    def near(a):
        cols = leaf_cols(a)
        p = points_v[:, cols] * SCALE
        top, rest = pair(p)
        norm = -0.5 * jnp.sum(p * p, axis=0, keepdims=True)
        n1 = norm.astype(BF16).astype(F32)
        n2 = (norm - n1).astype(BF16).astype(F32)
        n3 = norm - n1 - n2
        row = lax.broadcasted_iota(jnp.int32, (16, LEAF), 0)
        one = jnp.where(row < 6, 1.0, 0.0)
        left = jnp.where(row == 0, n1, jnp.where(row == 1, n2, jnp.where(row == 2, n3, one)))
        right = jnp.where(row == 3, n1, jnp.where(row == 4, n2, jnp.where(row == 5, n3, one)))
        pad = jnp.zeros((48, LEAF), BF16)
        a1 = jnp.concatenate([top, rest, top, left.astype(BF16), pad], axis=0)
        a2 = jnp.concatenate([top, top, rest, right.astype(BF16), pad], axis=0)
        power = lax.dot_general(a1, a2, (((0,), (0,)), ((), ())), preferred_element_type=F32)
        block = jnp.exp2(power).astype(BF16)
        rhs = x_v[:, cols]
        total = jnp.dot(rhs, block, preferred_element_type=F32) + rhs.astype(F32)
        high = jnp.broadcast_to(order_row(a) // LOW, (16, LEAF))
        for h in range(HIGH):
            mask_v[h, :, cols] = jnp.where(high == h, 1.0, 0.0).astype(BF16)
        low = jnp.broadcast_to(order_row(a) % LOW, (128, LEAF)).T
        place = lax.broadcasted_iota(jnp.int32, (LEAF, 128), 1)
        hot = [jnp.where(low == place + i * 128, 1.0, 0.0).astype(BF16) for i in range(2)]
        hot = jnp.concatenate(hot, axis=1)
        hot_v[cols, :] = hot
        both = jnp.dot(spread(a, pair(total)), hot, preferred_element_type=F32)
        for h in range(HIGH):
            at = 2 * h * COLS
            piece = both[at : at + COLS] + both[at + COLS : at + 2 * COLS]
            out_h[:, h * LOW : (h + 1) * LOW] += piece

    def nears(i, carry):
        near(2 * i)
        near(2 * i + 1)
        return carry

    ld_points.wait()
    out_h[...] = jnp.zeros_like(out_h)
    lax.fori_loop(0, 1, nears, 0)

    got_y = []
    for i in range(6):
        m = 3 - i // 2
        peer = dict(dy=m, dc=i % 2)
        src = half_v.at[0 if m == 1 else 1, flip(c, i % 2)]
        got_y.append(send_one(src, y_in.at[i], 1 + i, peer))
    lower = [peer for peer in PLANE if peer["dx"]]
    for i, peer in enumerate(lower):
        src = quart_v.at[0 if peer["dx"] == 1 else 1, quarter(**peer)]
        send(src, low_in.at[i], low_send, low_recv, peer)

    lax.fori_loop(1, 2, nears, 0)

    pltpu.make_async_copy(plane_in, plane_in, plane_recv).wait()
    s5 = jnp.sum(plane_in[...], axis=0) + quart_v[2, quarter()]
    l6 = times(s5, p_v[5])
    l7 = times(l6, p_v[6])
    z_out[0] = s5
    z_out[1] = l6
    z_out[2] = l7
    got_z = []
    for m in FAR_Z:
        got_z.append(send_one(z_out.at[m.bit_length() - 1], z_in.at[m - 1], 7 + m, dict(dz=m)))

    ld_qb.wait()

    def q_of(level):
        return qb_v[level, 0]

    def b_of(level):
        return qb_v[level, 1]

    m7 = jnp.dot(b_of(7), q_of(6), preferred_element_type=F32)
    both = jnp.dot(
        jnp.concatenate([halves(m7), b_of(6)], axis=0), q_of(5), preferred_element_type=F32
    )
    m7 = both[:RANK] + both[RANK : 2 * RANK]
    m6 = both[2 * RANK :]
    both = jnp.dot(
        jnp.concatenate([halves(m7), halves(m6), b_of(5)], axis=0), q_of(4), preferred_element_type=F32
    )
    m7 = both[:RANK] + both[RANK : 2 * RANK]
    m6 = both[2 * RANK : 3 * RANK] + both[3 * RANK : 4 * RANK]
    m5 = both[4 * RANK :]
    for i, mat in enumerate((m7, m6, m5)):
        mat = times(mat, q_of(3))
        m_top[i * RANK : (i + 1) * RANK], m_rest[i * RANK : (i + 1) * RANK] = pair(mat)

    ld_links.wait()
    for m in range(8):
        cpl[m] = times(xh0[m ^ 1], links_v[m // 2, m % 2])
    for m in range(4):
        cpl[8 + m] = times(xh1[m ^ 1], links_v[4 + m // 2, m % 2])
    for m in range(2):
        cpl[12 + m] = times(xh2[m ^ 1], links_v[6, m])

    for copy in got_y:
        copy.wait_recv()
    sib2 = (y_in[0] + y_in[1]) + (y_in[2] + y_in[3])
    sib1 = y_in[4] + y_in[5]
    e = times(times(sib2, b_of(2)), q_of(1)) + times(sib1, b_of(1))
    e_v[c] = e
    got_e = send_one(e_v.at[c], e_v.at[c], 15, core)

    pltpu.make_async_copy(low_in, low_in, low_recv).wait()
    sib3 = jnp.zeros((4, RANK), F32)
    sib4 = jnp.zeros((4, RANK), F32)
    for i, peer in enumerate(lower):
        if peer["dx"] == 1:
            sib3 = sib3 + low_in[i]
        else:
            sib4 = sib4 + low_in[i]
    c34 = times(times(sib4, b_of(4)), q_of(3)) + times(sib3, b_of(3))

    ld_down.wait()
    t = times(jnp.dot(q_of(2), q_of(1), preferred_element_type=F32), q_of(0))
    for m in range(2):
        w1_v[m] = times(t, down_v[12 + m])

    for m in range(4):
        w1_v[2 + m] = times(w1_v[m // 2], down_v[8 + m])
    for m in range(8):
        w_top[m], w_rest[m] = pair(times(w1_v[2 + m // 2], down_v[m]))
    lax.fori_loop(2, 3, nears, 0)

    for copy in got_z:
        copy.wait_recv()
    sib5 = z_in[0]
    sib6 = z_in[1] + z_in[2]
    sib7 = (z_in[3] + z_in[4]) + (z_in[5] + z_in[6])
    y3 = times_pair(jnp.concatenate([sib7, sib6, sib5], axis=1), m_top[...], m_rest[...]) + c34
    mine = quarter()
    y3_v[mine] = y3
    got_y3 = []
    for i, peer in enumerate([p for p in PLANE if p["dx"] == 0]):
        got_y3.append(send_one(y3_v.at[mine], y3_v.at[mine], 16 + i, peer))

    got_sib0.wait_recv()
    got_e.wait_recv()
    current = [times(sib0[...], b_of(0)) + times(e_v[...].reshape(COLS, RANK), q_of(0))]
    for number, first in ((2, 12), (4, 8), (8, 0)):
        current = [
            times(current[m // 2], down_v[first + m]) + cpl[first + m] for m in range(number)
        ]
    for m in range(8):
        g_v[m] = current[m]
    lax.fori_loop(3, 4, nears, 0)
    pltpu.make_async_copy(plane_in, plane_in, plane_send).wait()
    pltpu.make_async_copy(low_in, low_in, low_send).wait()
    for copy in sends[:-7]:
        copy.wait_send()

    for copy in got_y3:
        copy.wait_recv()
    y3 = jnp.concatenate([y3_v[i] for i in range(8)], axis=0)

    for a in range(LEAVES):
        cols = slice(a * LEAF, (a + 1) * LEAF)
        far = (times_pair(y3, w_top[a], w_rest[a]) + g_v[a]).astype(BF16)
        far = lax.dot_general(
            far, basis_v[cols, :], (((1,), (1,)), ((), ())), preferred_element_type=F32
        ).astype(BF16)
        for h in range(HIGH):
            mask = mask_v[h, :, cols]
            for i in range(2):
                at = h * COLS + 16 * i
                zs_v[at : at + 16, cols] = far[16 * i : 16 * i + 16] * mask
    def collect(i, carry):
        rows = pl.ds(pl.multiple_of(i * 256, 256), 256)
        total = jnp.dot(zs_v[rows, :], hot_v[...], preferred_element_type=F32)
        for h in range(8):
            cols = pl.ds(pl.multiple_of((i * 8 + h) * LOW, LOW), LOW)
            out_h[:, cols] += total[h * COLS : (h + 1) * COLS]
        return carry

    lax.fori_loop(0, 2, collect, 0)
    for copy in sends[-7:]:
        copy.wait_send()


def on_device(
    points, leaf_basis, right_sides, leaf_order, local_up, local_down, local_links, upper_nodes
):
    vm = pltpu.VMEM
    dma = pltpu.SemaphoreType.DMA
    scratch = [
        vm((DIMS, PTS), F32),
        vm((PTS, RANK), BF16),
        vm((COLS, PTS), BF16),
        vm((32, 128), jnp.int32),
        vm((14, RANK, RANK), BF16),
        vm((14, RANK, RANK), BF16),
        vm((7, 2, RANK, RANK), BF16),
        vm((8, RANK, RANK), BF16),
        vm((8, 2, RANK, RANK), BF16),
        vm((HIGH * COLS, LOW), BF16),
        vm((PTS, LOW), BF16),
        vm((HIGH, 16, PTS), BF16),
        vm((HIGH * COLS, PTS), BF16),
        vm((COLS, PTS), BF16),
        vm((8, COLS, RANK), F32),
        vm((4, COLS, RANK), F32),
        vm((2, COLS, RANK), F32),
        vm((14, COLS, RANK), F32),
        vm((COLS, RANK), F32),
        vm((COLS, RANK), F32),
        vm((2, 2, 16, RANK), F32),
        vm((3, 8, 4, RANK), F32),
        vm((31, 4, RANK), F32),
        vm((24, 4, RANK), F32),
        vm((6, 16, RANK), F32),
        vm((2, 16, RANK), F32),
        vm((3, 4, RANK), F32),
        vm((7, 4, RANK), F32),
        vm((8, 4, RANK), F32),
        vm((3 * RANK, RANK), BF16),
        vm((3 * RANK, RANK), BF16),
        vm((8, RANK, RANK), BF16),
        vm((8, RANK, RANK), BF16),
        vm((6, RANK, RANK), F32),
        vm((8, COLS, RANK), F32),
        dma((9,)),
        dma((23,)),
        dma((23,)),
        dma,
        dma,
        dma,
        dma,
    ]
    operands = [
        pltpu.with_memory_space_constraint(operand, pltpu.HBM)
        for operand in (
            points, leaf_basis, right_sides, leaf_order.reshape(32, 128), local_up, local_down,
            local_links, upper_nodes.reshape(8, 3, RANK, RANK),
        )
    ]
    return pl.pallas_call(
        kernel,
        out_shape=pltpu.VMEM((COLS, PTS), F32),
        in_specs=[pl.BlockSpec(memory_space=pltpu.HBM)] * 8,
        out_specs=pl.BlockSpec(memory_space=pltpu.VMEM),
        scratch_shapes=scratch,
        compiler_params=pltpu.CompilerParams(
            collective_id=0, has_side_effects=True, vmem_limit_bytes=48 * 2**20
        ),
    )(*operands)


def solution(mesh):
    in_specs = (
        P(None, ("leaf", "wide")),
        P(("leaf", "wide"), None),
        P(None, ("leaf", "wide")),
        P(("leaf", "wide")),
        P(("leaf", "wide"), None, None),
        P(("leaf", "wide"), None, None),
        P(("leaf", "wide"), None, None, None),
        P(("leaf", "wide"), None, None, None, None),
    )
    out_specs = P(None, ("leaf", "wide"))
    return jax.shard_map(
        on_device, mesh=mesh, in_specs=in_specs, out_specs=out_specs, check_vma=False
    )
```

```python
import math

import jax
import jax.numpy as jnp
from jax import lax
from jax.experimental import pallas as pl
from jax.experimental.pallas import tpu as pltpu
from jax.sharding import PartitionSpec as P

MESH = pl.DeviceIdType.MESH
F32 = jnp.float32
BF16 = jnp.bfloat16
LEAVES = 8
LEAF = 512
RANK = 256
COLS = 32
PTS = 4096
DIMS = 64
LOW = 256
HIGH = PTS // LOW
SCALE = math.sqrt(math.log2(math.e) * 4.0 / DIMS)


def flip(value, mask):
    for bit in (1, 2, 4):
        if mask & bit:
            value = value + bit * (1 - 2 * ((value // bit) % 2))
    return value


def halves(values):
    top = values.astype(BF16)
    rest = (values - top.astype(F32)).astype(BF16)
    return jnp.concatenate([top, rest], axis=0)


def times(values, matrix):
    rows = values.shape[0]
    both = jnp.dot(halves(values), matrix, preferred_element_type=F32)
    return both[:rows] + both[rows:]


def pair(values):
    top = values.astype(BF16)
    return top, (values - top.astype(F32)).astype(BF16)


def times_pair(values, top, rest):
    rows = values.shape[0]
    parts = halves(values)
    both = jnp.dot(parts, top, preferred_element_type=F32)
    return both[:rows] + both[rows:] + jnp.dot(parts[:rows], rest, preferred_element_type=F32)


PLANE = sorted(
    (
        dict(dx=dx, dy=dy, dc=dc)
        for dx in range(4)
        for dy in range(4)
        for dc in range(2)
        if dx or dy or dc
    ),
    key=lambda p: -(p["dx"] > 0) - (p["dx"] == 2) - (p["dy"] > 0) - (p["dy"] == 2),
)
FAR_Z = (4, 3, 5, 2, 6, 7, 1)


def kernel(
    points_h, basis_h, rhs_h, order_h, up_h, down_h, links_h, upper_h,
    out_h,
    points_v, basis_v, rhs_v, order_v, up_v, down_v, links_v, p_v, qb_v,
    stack_v, hot_v, mask_v, zs_v, x_v,
    xh0, xh1, xh2, cpl, root_v, sib0, half_v, quart_v, plane_in, low_in, y_in,
    e_v, z_out, z_in, y3_v, m_top, m_rest, w_top, w_rest, w1_v, g_v,
    load_sem, one_send, one_recv, plane_send, plane_recv, low_send, low_recv,
):
    z = lax.axis_index("leaf")
    w = lax.axis_index("wide")
    c = w % 2
    y = (w // 2) % 4
    x = w // 8

    zs = [flip(z, m) for m in range(8)]
    xs = [flip(x, m) * 8 for m in range(4)]
    ys = [flip(y, m) for m in range(4)]
    cs = [c, 1 - c]
    yc = [[ys[m] * 2 + cs[i] for i in range(2)] for m in range(4)]
    quarters = [[cs[i] * 4 + ys[m] for i in range(2)] for m in range(4)]

    def device(dz=0, dx=0, dy=0, dc=0):
        return (zs[dz], xs[dx] + yc[dy][dc])

    def quarter(dx=0, dy=0, dc=0):
        return quarters[dy][dc]

    def load(i, src, dst):
        copy = pltpu.make_async_copy(src, dst, load_sem.at[i])
        copy.start()
        return copy

    ld_order = load(0, order_h, order_v)
    ld_rhs = load(1, rhs_h, rhs_v)
    ld_basis = load(2, basis_h, basis_v)
    ld_up = load(3, up_h, up_v)
    ld_p = load(4, upper_h.at[:, 0], p_v)

    barrier = pltpu.get_barrier_semaphore()
    peers = PLANE + [dict(dz=m) for m in FAR_Z]
    for peer in peers:
        pl.semaphore_signal(barrier, inc=1, device_id=device(**peer), device_id_type=MESH)

    sends = []

    def send(src, dst, send_sem, recv_sem, peer):
        copy = pltpu.make_async_remote_copy(
            src_ref=src,
            dst_ref=dst,
            send_sem=send_sem,
            recv_sem=recv_sem,
            device_id=device(**peer),
            device_id_type=MESH,
        )
        copy.start()
        return copy

    def send_one(src, dst, slot, peer):
        copy = send(src, dst, one_send.at[slot], one_recv.at[slot], peer)
        sends.append(copy)
        return copy

    def order_row(a):
        rows = order_v[pl.ds(a * 4, 4), :]
        return jnp.concatenate([rows[i : i + 1] for i in range(4)], axis=1)

    def leaf_cols(a):
        return pl.ds(pl.multiple_of(a * LEAF, LEAF), LEAF)

    ld_order.wait()
    ld_rhs.wait()
    for h in range(HIGH):
        stack_v[h * COLS : (h + 1) * COLS, :] = rhs_v[:, h * LOW : (h + 1) * LOW]
    def gather(a):
        row = order_row(a)
        low = row % LOW
        high = jnp.broadcast_to(row // LOW, (8, LEAF))
        place = lax.broadcasted_iota(jnp.int32, (LOW, LEAF), 0)
        hot = jnp.where(place == low, 1.0, 0.0).astype(BF16)
        every = jnp.dot(stack_v[...], hot, preferred_element_type=F32)
        every = every.reshape(HIGH, COLS // 8, 8, LEAF)
        found = every[0]
        for h in range(1, HIGH):
            found = jnp.where((high == h)[None], every[h], found)
        x_v[:, leaf_cols(a)] = found.reshape(COLS, LEAF).astype(BF16)

    def gathers(i, carry):
        for j in range(4):
            gather(4 * i + j)
        return carry

    lax.fori_loop(0, LEAVES // 4, gathers, 0)
    ld_basis.wait()
    ld_up.wait()
    ld_p.wait()
    ld_points = load(5, points_h, points_v)
    ld_qb = load(8, upper_h.at[:, 1:], qb_v)
    ld_links = load(6, links_h, links_v)
    ld_down = load(7, down_h, down_v)
    p01 = jnp.dot(p_v[0], p_v[1], preferred_element_type=F32)
    p23 = jnp.dot(p_v[2], p_v[3], preferred_element_type=F32)
    for a in range(LEAVES):
        cols = slice(a * LEAF, (a + 1) * LEAF)
        xh0[a] = jnp.dot(x_v[:, cols], basis_v[cols, :], preferred_element_type=F32)

    def lift_pair(ref, n, first):
        both = jnp.concatenate([ref[2 * n], ref[2 * n + 1]], axis=1)
        mats = up_v[first + 2 * n : first + 2 * n + 2].reshape(2 * RANK, RANK)
        return times(both, mats)

    for n in range(4):
        xh1[n] = lift_pair(xh0, n, 0)
    p03 = times_pair(p01, *pair(p23))
    for n in range(2):
        xh2[n] = lift_pair(xh1, n, 8)
    p04 = pair(times(p03, p_v[4]))
    root = lift_pair(xh2, 0, 12)
    lift5 = times_pair(root, *p04)
    for q in range(8):
        quart_v[2, q] = lift5[q * 4 : q * 4 + 4]
    pl.semaphore_wait(barrier, len(peers))
    for i, peer in enumerate(PLANE):
        send(quart_v.at[2, quarter(**peer)], plane_in.at[i], plane_send, plane_recv, peer)
    root_v[...] = root
    lift = [root]
    for level in range(4):
        lift.append(times(lift[-1], p_v[level]))
    core = dict(dc=1)
    got_sib0 = send_one(root_v, sib0, 0, core)
    for level in (1, 2):
        for half in range(2):
            half_v[level - 1, half] = lift[level][half * 16 : half * 16 + 16]
    for level in (3, 4):
        for q in range(8):
            quart_v[level - 3, q] = lift[level][q * 4 : q * 4 + 4]

    def spread(a, parts):
        rows = []
        for h in range(HIGH):
            mask = mask_v[h, :, leaf_cols(a)]
            mask = jnp.concatenate([mask, mask], axis=0)
            rows += [part * mask for part in parts]
        return jnp.concatenate(rows, axis=0)

    def near(a):
        cols = leaf_cols(a)
        p = points_v[:, cols] * SCALE
        top, rest = pair(p)
        norm = -0.5 * jnp.sum(p * p, axis=0, keepdims=True)
        n1 = norm.astype(BF16).astype(F32)
        n2 = (norm - n1).astype(BF16).astype(F32)
        n3 = norm - n1 - n2
        row = lax.broadcasted_iota(jnp.int32, (16, LEAF), 0)
        one = jnp.where(row < 6, 1.0, 0.0)
        left = jnp.where(row == 0, n1, jnp.where(row == 1, n2, jnp.where(row == 2, n3, one)))
        right = jnp.where(row == 3, n1, jnp.where(row == 4, n2, jnp.where(row == 5, n3, one)))
        pad = jnp.zeros((48, LEAF), BF16)
        a1 = jnp.concatenate([top, rest, top, left.astype(BF16), pad], axis=0)
        a2 = jnp.concatenate([top, top, rest, right.astype(BF16), pad], axis=0)
        power = lax.dot_general(a1, a2, (((0,), (0,)), ((), ())), preferred_element_type=F32)
        block = jnp.exp2(power).astype(BF16)
        rhs = x_v[:, cols]
        total = jnp.dot(rhs, block, preferred_element_type=F32) + rhs.astype(F32)
        high = jnp.broadcast_to(order_row(a) // LOW, (16, LEAF))
        for h in range(HIGH):
            mask_v[h, :, cols] = jnp.where(high == h, 1.0, 0.0).astype(BF16)
        low = jnp.broadcast_to(order_row(a) % LOW, (128, LEAF)).T
        place = lax.broadcasted_iota(jnp.int32, (LEAF, 128), 1)
        hot = [jnp.where(low == place + i * 128, 1.0, 0.0).astype(BF16) for i in range(2)]
        hot = jnp.concatenate(hot, axis=1)
        hot_v[cols, :] = hot
        both = jnp.dot(spread(a, pair(total)), hot, preferred_element_type=F32)
        for h in range(HIGH):
            at = 2 * h * COLS
            piece = both[at : at + COLS] + both[at + COLS : at + 2 * COLS]
            out_h[:, h * LOW : (h + 1) * LOW] += piece

    def nears(i, carry):
        near(2 * i)
        near(2 * i + 1)
        return carry

    ld_points.wait()
    out_h[...] = jnp.zeros_like(out_h)
    lax.fori_loop(0, 1, nears, 0)

    got_y = []
    for i in range(6):
        m = 3 - i // 2
        peer = dict(dy=m, dc=i % 2)
        src = half_v.at[0 if m == 1 else 1, cs[i % 2]]
        got_y.append(send_one(src, y_in.at[i], 1 + i, peer))
    lower = [peer for peer in PLANE if peer["dx"]]
    for i, peer in enumerate(lower):
        src = quart_v.at[0 if peer["dx"] == 1 else 1, quarter(**peer)]
        send(src, low_in.at[i], low_send, low_recv, peer)

    lax.fori_loop(1, 2, nears, 0)

    p56 = pair(jnp.dot(p_v[5], p_v[6], preferred_element_type=F32))
    pltpu.make_async_copy(plane_in, plane_in, plane_recv).wait()
    s5 = jnp.sum(plane_in[...], axis=0) + quart_v[2, quarter()]
    l6 = times(s5, p_v[5])
    l7 = times_pair(s5, *p56)
    z_out[0] = s5
    z_out[1] = l6
    z_out[2] = l7
    got_z = []
    for m in FAR_Z:
        got_z.append(send_one(z_out.at[m.bit_length() - 1], z_in.at[m - 1], 7 + m, dict(dz=m)))

    ld_qb.wait()

    def q_of(level):
        return qb_v[level, 0]

    def b_of(level):
        return qb_v[level, 1]

    m7 = jnp.dot(b_of(7), q_of(6), preferred_element_type=F32)
    both = jnp.dot(
        jnp.concatenate([halves(m7), b_of(6)], axis=0), q_of(5), preferred_element_type=F32
    )
    m7 = both[:RANK] + both[RANK : 2 * RANK]
    m6 = both[2 * RANK :]
    both = jnp.dot(
        jnp.concatenate([halves(m7), halves(m6), b_of(5)], axis=0), q_of(4), preferred_element_type=F32
    )
    m7 = both[:RANK] + both[RANK : 2 * RANK]
    m6 = both[2 * RANK : 3 * RANK] + both[3 * RANK : 4 * RANK]
    m5 = both[4 * RANK :]
    for i, mat in enumerate((m7, m6, m5)):
        mat = times(mat, q_of(3))
        m_top[i * RANK : (i + 1) * RANK], m_rest[i * RANK : (i + 1) * RANK] = pair(mat)

    ld_links.wait()
    for m in range(8):
        cpl[m] = times(xh0[m ^ 1], links_v[m // 2, m % 2])
    for m in range(4):
        cpl[8 + m] = times(xh1[m ^ 1], links_v[4 + m // 2, m % 2])
    for m in range(2):
        cpl[12 + m] = times(xh2[m ^ 1], links_v[6, m])

    for copy in got_y:
        copy.wait_recv()
    sib2 = (y_in[0] + y_in[1]) + (y_in[2] + y_in[3])
    sib1 = y_in[4] + y_in[5]
    e = times(times(sib2, b_of(2)), q_of(1)) + times(sib1, b_of(1))
    e_v[c] = e
    got_e = send_one(e_v.at[c], e_v.at[c], 15, core)

    pltpu.make_async_copy(low_in, low_in, low_recv).wait()
    sib3 = jnp.zeros((4, RANK), F32)
    sib4 = jnp.zeros((4, RANK), F32)
    for i, peer in enumerate(lower):
        if peer["dx"] == 1:
            sib3 = sib3 + low_in[i]
        else:
            sib4 = sib4 + low_in[i]
    c34 = times(times(sib4, b_of(4)), q_of(3)) + times(sib3, b_of(3))

    ld_down.wait()
    t = times(jnp.dot(q_of(2), q_of(1), preferred_element_type=F32), q_of(0))
    for m in range(2):
        w1_v[m] = times(t, down_v[12 + m])

    for m in range(4):
        w1_v[2 + m] = times(w1_v[m // 2], down_v[8 + m])
    for m in range(8):
        w_top[m], w_rest[m] = pair(times(w1_v[2 + m // 2], down_v[m]))
    lax.fori_loop(2, 3, nears, 0)

    for copy in got_z:
        copy.wait_recv()
    sib5 = z_in[0]
    sib6 = z_in[1] + z_in[2]
    sib7 = (z_in[3] + z_in[4]) + (z_in[5] + z_in[6])
    y3 = times_pair(jnp.concatenate([sib7, sib6, sib5], axis=1), m_top[...], m_rest[...]) + c34
    mine = quarter()
    y3_v[mine] = y3
    got_y3 = []
    for i, peer in enumerate([p for p in PLANE if p["dx"] == 0]):
        got_y3.append(send_one(y3_v.at[mine], y3_v.at[mine], 16 + i, peer))

    got_sib0.wait_recv()
    got_e.wait_recv()
    current = [times(sib0[...], b_of(0)) + times(e_v[...].reshape(COLS, RANK), q_of(0))]
    for number, first in ((2, 12), (4, 8), (8, 0)):
        current = [
            times(current[m // 2], down_v[first + m]) + cpl[first + m] for m in range(number)
        ]
    for m in range(8):
        g_v[m] = current[m]
    lax.fori_loop(3, 4, nears, 0)
    pltpu.make_async_copy(plane_in, plane_in, plane_send).wait()
    pltpu.make_async_copy(low_in, low_in, low_send).wait()
    for copy in sends[:-7]:
        copy.wait_send()

    for copy in got_y3:
        copy.wait_recv()
    y3 = jnp.concatenate([y3_v[i] for i in range(8)], axis=0)

    for a in range(LEAVES):
        cols = slice(a * LEAF, (a + 1) * LEAF)
        far = (times_pair(y3, w_top[a], w_rest[a]) + g_v[a]).astype(BF16)
        far = lax.dot_general(
            far, basis_v[cols, :], (((1,), (1,)), ((), ())), preferred_element_type=F32
        ).astype(BF16)
        for h in range(HIGH):
            mask = mask_v[h, :, cols]
            for i in range(2):
                at = h * COLS + 16 * i
                zs_v[at : at + 16, cols] = far[16 * i : 16 * i + 16] * mask
    def collect(i, carry):
        rows = pl.ds(pl.multiple_of(i * 512, 512), 512)
        total = jnp.dot(zs_v[rows, :], hot_v[...], preferred_element_type=F32)
        for h in range(HIGH):
            cols = pl.ds(pl.multiple_of((i * HIGH + h) * LOW, LOW), LOW)
            out_h[:, cols] += total[h * COLS : (h + 1) * COLS]
        return carry

    lax.fori_loop(0, 1 + w // 32, collect, 0)
    for copy in sends[-7:]:
        copy.wait_send()


def on_device(
    points, leaf_basis, right_sides, leaf_order, local_up, local_down, local_links, upper_nodes
):
    vm = pltpu.VMEM
    dma = pltpu.SemaphoreType.DMA
    scratch = [
        vm((DIMS, PTS), F32),
        vm((PTS, RANK), BF16),
        vm((COLS, PTS), BF16),
        vm((32, 128), jnp.int32),
        vm((14, RANK, RANK), BF16),
        vm((14, RANK, RANK), BF16),
        vm((7, 2, RANK, RANK), BF16),
        vm((8, RANK, RANK), BF16),
        vm((8, 2, RANK, RANK), BF16),
        vm((HIGH * COLS, LOW), BF16),
        vm((PTS, LOW), BF16),
        vm((HIGH, 16, PTS), BF16),
        vm((HIGH * COLS, PTS), BF16),
        vm((COLS, PTS), BF16),
        vm((8, COLS, RANK), F32),
        vm((4, COLS, RANK), F32),
        vm((2, COLS, RANK), F32),
        vm((14, COLS, RANK), F32),
        vm((COLS, RANK), F32),
        vm((COLS, RANK), F32),
        vm((2, 2, 16, RANK), F32),
        vm((3, 8, 4, RANK), F32),
        vm((31, 4, RANK), F32),
        vm((24, 4, RANK), F32),
        vm((6, 16, RANK), F32),
        vm((2, 16, RANK), F32),
        vm((3, 4, RANK), F32),
        vm((7, 4, RANK), F32),
        vm((8, 4, RANK), F32),
        vm((3 * RANK, RANK), BF16),
        vm((3 * RANK, RANK), BF16),
        vm((8, RANK, RANK), BF16),
        vm((8, RANK, RANK), BF16),
        vm((6, RANK, RANK), F32),
        vm((8, COLS, RANK), F32),
        dma((9,)),
        dma((23,)),
        dma((23,)),
        dma,
        dma,
        dma,
        dma,
    ]
    operands = [
        pltpu.with_memory_space_constraint(operand, pltpu.HBM)
        for operand in (
            points, leaf_basis, right_sides, leaf_order.reshape(32, 128), local_up, local_down,
            local_links, upper_nodes.reshape(8, 3, RANK, RANK),
        )
    ]
    return pl.pallas_call(
        kernel,
        out_shape=pltpu.VMEM((COLS, PTS), F32),
        in_specs=[pl.BlockSpec(memory_space=pltpu.HBM)] * 8,
        out_specs=pl.BlockSpec(memory_space=pltpu.VMEM),
        scratch_shapes=scratch,
        compiler_params=pltpu.CompilerParams(
            collective_id=0, has_side_effects=True, vmem_limit_bytes=48 * 2**20
        ),
    )(*operands)


def solution(mesh):
    in_specs = (
        P(None, ("leaf", "wide")),
        P(("leaf", "wide"), None),
        P(None, ("leaf", "wide")),
        P(("leaf", "wide")),
        P(("leaf", "wide"), None, None),
        P(("leaf", "wide"), None, None),
        P(("leaf", "wide"), None, None, None),
        P(("leaf", "wide"), None, None, None, None),
    )
    out_specs = P(None, ("leaf", "wide"))
    return jax.shard_map(
        on_device, mesh=mesh, in_specs=in_specs, out_specs=out_specs, check_vma=False
    )
```

```python
import math

import jax
import jax.numpy as jnp
from jax import lax
from jax.experimental import pallas as pl
from jax.experimental.pallas import tpu as pltpu
from jax.sharding import PartitionSpec as P

MESH = pl.DeviceIdType.MESH
F32 = jnp.float32
BF16 = jnp.bfloat16
LEAVES = 8
LEAF = 512
RANK = 256
COLS = 32
PTS = 4096
DIMS = 64
LOW = 256
HIGH = PTS // LOW
SCALE = math.sqrt(math.log2(math.e) * 4.0 / DIMS)


def flip(value, mask):
    for bit in (1, 2, 4):
        if mask & bit:
            value = value + bit * (1 - 2 * ((value // bit) % 2))
    return value


def halves(values):
    top = values.astype(BF16)
    rest = (values - top.astype(F32)).astype(BF16)
    return jnp.concatenate([top, rest], axis=0)


def times(values, matrix):
    rows = values.shape[0]
    both = jnp.dot(halves(values), matrix, preferred_element_type=F32)
    return both[:rows] + both[rows:]


def pair(values):
    top = values.astype(BF16)
    return top, (values - top.astype(F32)).astype(BF16)


def times_pair(values, top, rest):
    rows = values.shape[0]
    parts = halves(values)
    both = jnp.dot(parts, top, preferred_element_type=F32)
    return both[:rows] + both[rows:] + jnp.dot(parts[:rows], rest, preferred_element_type=F32)


PLANE = sorted(
    (
        dict(dx=dx, dy=dy, dc=dc)
        for dx in range(4)
        for dy in range(4)
        for dc in range(2)
        if dx or dy or dc
    ),
    key=lambda p: -(p["dx"] > 0) - (p["dx"] == 2) - (p["dy"] > 0) - (p["dy"] == 2),
)
FAR_Z = (4, 3, 5, 2, 6, 7, 1)


def kernel(
    points_h, basis_h, rhs_h, order_h, up_h, down_h, links_h, upper_h,
    out_h,
    points_v, basis_v, rhs_v, order_v, up_v, down_v, links_v, p_v, qb_v,
    stack_v, hot_v, mask_v, zs_v, x_v,
    xh0, xh1, xh2, cpl, root_v, sib0, half_v, quart_v, plane_in, low_in, y_in,
    e_v, z_out, z_in, y3_v, m_top, m_rest, w_top, w_rest, w1_v, g_v,
    load_sem, one_send, one_recv, plane_send, plane_recv, low_send, low_recv,
):
    z = lax.axis_index("leaf")
    w = lax.axis_index("wide")
    c = w % 2
    y = (w // 2) % 4
    x = w // 8

    zs = [flip(z, m) for m in range(8)]
    xs = [flip(x, m) * 8 for m in range(4)]
    ys = [flip(y, m) for m in range(4)]
    cs = [c, 1 - c]
    yc = [[ys[m] * 2 + cs[i] for i in range(2)] for m in range(4)]
    quarters = [[cs[i] * 4 + ys[m] for i in range(2)] for m in range(4)]

    def device(dz=0, dx=0, dy=0, dc=0):
        return (zs[dz], xs[dx] + yc[dy][dc])

    def quarter(dx=0, dy=0, dc=0):
        return quarters[dy][dc]

    def load(i, src, dst):
        copy = pltpu.make_async_copy(src, dst, load_sem.at[i])
        copy.start()
        return copy

    ld_order = load(0, order_h, order_v)
    ld_rhs = load(1, rhs_h, rhs_v)
    ld_basis = load(2, basis_h, basis_v)
    ld_up = load(3, up_h, up_v)
    ld_p = load(4, upper_h.at[:, 0], p_v)

    barrier = pltpu.get_barrier_semaphore()
    peers = PLANE + [dict(dz=m) for m in FAR_Z]
    for peer in peers:
        pl.semaphore_signal(barrier, inc=1, device_id=device(**peer), device_id_type=MESH)

    sends = []

    def send(src, dst, send_sem, recv_sem, peer):
        copy = pltpu.make_async_remote_copy(
            src_ref=src,
            dst_ref=dst,
            send_sem=send_sem,
            recv_sem=recv_sem,
            device_id=device(**peer),
            device_id_type=MESH,
        )
        copy.start()
        return copy

    def send_one(src, dst, slot, peer):
        copy = send(src, dst, one_send.at[slot], one_recv.at[slot], peer)
        sends.append(copy)
        return copy

    def order_row(a):
        rows = order_v[pl.ds(a * 4, 4), :]
        return jnp.concatenate([rows[i : i + 1] for i in range(4)], axis=1)

    def leaf_cols(a):
        return pl.ds(pl.multiple_of(a * LEAF, LEAF), LEAF)

    ld_order.wait()
    ld_rhs.wait()
    for h in range(HIGH):
        stack_v[h * COLS : (h + 1) * COLS, :] = rhs_v[:, h * LOW : (h + 1) * LOW]
    def gather(a):
        row = order_row(a)
        low = row % LOW
        high = jnp.broadcast_to(row // LOW, (8, LEAF))
        place = lax.broadcasted_iota(jnp.int32, (LOW, LEAF), 0)
        hot = jnp.where(place == low, 1.0, 0.0).astype(BF16)
        every = jnp.dot(stack_v[...], hot, preferred_element_type=F32)
        every = every.reshape(HIGH, COLS // 8, 8, LEAF)
        found = every[0]
        for h in range(1, HIGH):
            found = jnp.where((high == h)[None], every[h], found)
        x_v[:, leaf_cols(a)] = found.reshape(COLS, LEAF).astype(BF16)

    def gathers(i, carry):
        for j in range(4):
            gather(4 * i + j)
        return carry

    lax.fori_loop(0, LEAVES // 4, gathers, 0)
    ld_basis.wait()
    ld_up.wait()
    ld_p.wait()
    ld_points = load(5, points_h, points_v)
    ld_qb = load(8, upper_h.at[:, 1:], qb_v)
    ld_links = load(6, links_h, links_v)
    ld_down = load(7, down_h, down_v)
    p01 = jnp.dot(p_v[0], p_v[1], preferred_element_type=F32)
    p23 = jnp.dot(p_v[2], p_v[3], preferred_element_type=F32)
    for a in range(LEAVES):
        cols = slice(a * LEAF, (a + 1) * LEAF)
        xh0[a] = jnp.dot(x_v[:, cols], basis_v[cols, :], preferred_element_type=F32)

    def lift_pair(ref, n, first):
        both = jnp.concatenate([ref[2 * n], ref[2 * n + 1]], axis=1)
        mats = up_v[first + 2 * n : first + 2 * n + 2].reshape(2 * RANK, RANK)
        return times(both, mats)

    for n in range(4):
        xh1[n] = lift_pair(xh0, n, 0)
    p03 = times_pair(p01, *pair(p23))
    for n in range(2):
        xh2[n] = lift_pair(xh1, n, 8)
    p04 = pair(times(p03, p_v[4]))
    root = lift_pair(xh2, 0, 12)
    lift5 = times_pair(root, *p04)
    for q in range(8):
        quart_v[2, q] = lift5[q * 4 : q * 4 + 4]
    pl.semaphore_wait(barrier, len(peers))
    for i, peer in enumerate(PLANE):
        send(quart_v.at[2, quarter(**peer)], plane_in.at[i], plane_send, plane_recv, peer)
    root_v[...] = root
    lift = [root]
    for level in range(4):
        lift.append(times(lift[-1], p_v[level]))
    core = dict(dc=1)
    got_sib0 = send_one(root_v, sib0, 0, core)
    for level in (1, 2):
        for half in range(2):
            half_v[level - 1, half] = lift[level][half * 16 : half * 16 + 16]
    for level in (3, 4):
        for q in range(8):
            quart_v[level - 3, q] = lift[level][q * 4 : q * 4 + 4]

    def spread(a, parts):
        rows = []
        for h in range(HIGH):
            mask = mask_v[h, :, leaf_cols(a)]
            mask = jnp.concatenate([mask, mask], axis=0)
            rows += [part * mask for part in parts]
        return jnp.concatenate(rows, axis=0)

    def near(a):
        cols = leaf_cols(a)
        p = points_v[:, cols] * SCALE
        top, rest = pair(p)
        norm = -0.5 * jnp.sum(p * p, axis=0, keepdims=True)
        n1 = norm.astype(BF16).astype(F32)
        n2 = (norm - n1).astype(BF16).astype(F32)
        n3 = norm - n1 - n2
        row = lax.broadcasted_iota(jnp.int32, (16, LEAF), 0)
        one = jnp.where(row < 6, 1.0, 0.0)
        left = jnp.where(row == 0, n1, jnp.where(row == 1, n2, jnp.where(row == 2, n3, one)))
        right = jnp.where(row == 3, n1, jnp.where(row == 4, n2, jnp.where(row == 5, n3, one)))
        pad = jnp.zeros((48, LEAF), BF16)
        a1 = jnp.concatenate([top, rest, top, left.astype(BF16), pad], axis=0)
        a2 = jnp.concatenate([top, top, rest, right.astype(BF16), pad], axis=0)
        power = lax.dot_general(a1, a2, (((0,), (0,)), ((), ())), preferred_element_type=F32)
        block = jnp.exp2(power).astype(BF16)
        rhs = x_v[:, cols]
        total = jnp.dot(rhs, block, preferred_element_type=F32) + rhs.astype(F32)
        high = jnp.broadcast_to(order_row(a) // LOW, (16, LEAF))
        for h in range(HIGH):
            mask_v[h, :, cols] = jnp.where(high == h, 1.0, 0.0).astype(BF16)
        low = jnp.broadcast_to(order_row(a) % LOW, (128, LEAF)).T
        place = lax.broadcasted_iota(jnp.int32, (LEAF, 128), 1)
        hot = [jnp.where(low == place + i * 128, 1.0, 0.0).astype(BF16) for i in range(2)]
        hot = jnp.concatenate(hot, axis=1)
        hot_v[cols, :] = hot
        both = jnp.dot(spread(a, pair(total)), hot, preferred_element_type=F32)
        for h in range(HIGH):
            at = 2 * h * COLS
            piece = both[at : at + COLS] + both[at + COLS : at + 2 * COLS]
            out_h[:, h * LOW : (h + 1) * LOW] += piece

    def nears(i, carry):
        near(2 * i)
        near(2 * i + 1)
        return carry

    ld_points.wait()
    out_h[...] = jnp.zeros_like(out_h)
    lax.fori_loop(0, 1, nears, 0)

    got_y = []
    for i in range(6):
        m = 3 - i // 2
        peer = dict(dy=m, dc=i % 2)
        src = half_v.at[0 if m == 1 else 1, cs[i % 2]]
        got_y.append(send_one(src, y_in.at[i], 1 + i, peer))
    lower = [peer for peer in PLANE if peer["dx"]]
    for i, peer in enumerate(lower):
        src = quart_v.at[0 if peer["dx"] == 1 else 1, quarter(**peer)]
        send(src, low_in.at[i], low_send, low_recv, peer)

    lax.fori_loop(1, 2, nears, 0)
    near(4)

    p56 = pair(jnp.dot(p_v[5], p_v[6], preferred_element_type=F32))
    pltpu.make_async_copy(plane_in, plane_in, plane_recv).wait()
    s5 = jnp.sum(plane_in[...], axis=0) + quart_v[2, quarter()]
    l6 = times(s5, p_v[5])
    l7 = times_pair(s5, *p56)
    z_out[0] = s5
    z_out[1] = l6
    z_out[2] = l7
    got_z = []
    for m in FAR_Z:
        got_z.append(send_one(z_out.at[m.bit_length() - 1], z_in.at[m - 1], 7 + m, dict(dz=m)))

    ld_qb.wait()

    def q_of(level):
        return qb_v[level, 0]

    def b_of(level):
        return qb_v[level, 1]

    m7 = jnp.dot(b_of(7), q_of(6), preferred_element_type=F32)
    both = jnp.dot(
        jnp.concatenate([halves(m7), b_of(6)], axis=0), q_of(5), preferred_element_type=F32
    )
    m7 = both[:RANK] + both[RANK : 2 * RANK]
    m6 = both[2 * RANK :]
    both = jnp.dot(
        jnp.concatenate([halves(m7), halves(m6), b_of(5)], axis=0), q_of(4), preferred_element_type=F32
    )
    m7 = both[:RANK] + both[RANK : 2 * RANK]
    m6 = both[2 * RANK : 3 * RANK] + both[3 * RANK : 4 * RANK]
    m5 = both[4 * RANK :]
    for i, mat in enumerate((m7, m6, m5)):
        mat = times(mat, q_of(3))
        m_top[i * RANK : (i + 1) * RANK], m_rest[i * RANK : (i + 1) * RANK] = pair(mat)

    ld_links.wait()
    for m in range(8):
        cpl[m] = times(xh0[m ^ 1], links_v[m // 2, m % 2])
    for m in range(4):
        cpl[8 + m] = times(xh1[m ^ 1], links_v[4 + m // 2, m % 2])
    for m in range(2):
        cpl[12 + m] = times(xh2[m ^ 1], links_v[6, m])

    ld_down.wait()
    t = times(jnp.dot(q_of(2), q_of(1), preferred_element_type=F32), q_of(0))
    for m in range(2):
        w1_v[m] = times(t, down_v[12 + m])

    for m in range(4):
        w1_v[2 + m] = times(w1_v[m // 2], down_v[8 + m])
    for m in range(8):
        w_top[m], w_rest[m] = pair(times(w1_v[2 + m // 2], down_v[m]))
    for copy in got_y:
        copy.wait_recv()
    sib2 = (y_in[0] + y_in[1]) + (y_in[2] + y_in[3])
    sib1 = y_in[4] + y_in[5]
    e = times(times(sib2, b_of(2)), q_of(1)) + times(sib1, b_of(1))
    e_v[c] = e
    got_e = send_one(e_v.at[c], e_v.at[c], 15, core)

    pltpu.make_async_copy(low_in, low_in, low_recv).wait()
    sib3 = jnp.zeros((4, RANK), F32)
    sib4 = jnp.zeros((4, RANK), F32)
    for i, peer in enumerate(lower):
        if peer["dx"] == 1:
            sib3 = sib3 + low_in[i]
        else:
            sib4 = sib4 + low_in[i]
    c34 = times(times(sib4, b_of(4)), q_of(3)) + times(sib3, b_of(3))


    for copy in got_z:
        copy.wait_recv()
    sib5 = z_in[0]
    sib6 = z_in[1] + z_in[2]
    sib7 = (z_in[3] + z_in[4]) + (z_in[5] + z_in[6])
    y3 = times_pair(jnp.concatenate([sib7, sib6, sib5], axis=1), m_top[...], m_rest[...]) + c34
    mine = quarter()
    y3_v[mine] = y3
    got_y3 = []
    for i, peer in enumerate([p for p in PLANE if p["dx"] == 0]):
        got_y3.append(send_one(y3_v.at[mine], y3_v.at[mine], 16 + i, peer))

    got_sib0.wait_recv()
    got_e.wait_recv()
    current = [times(sib0[...], b_of(0)) + times(e_v[...].reshape(COLS, RANK), q_of(0))]
    for number, first in ((2, 12), (4, 8), (8, 0)):
        current = [
            times(current[m // 2], down_v[first + m]) + cpl[first + m] for m in range(number)
        ]
    for m in range(8):
        g_v[m] = current[m]
    lax.fori_loop(3, 4, nears, 0)
    near(5)
    pltpu.make_async_copy(plane_in, plane_in, plane_send).wait()
    pltpu.make_async_copy(low_in, low_in, low_send).wait()
    for copy in sends[:-7]:
        copy.wait_send()

    for copy in got_y3:
        copy.wait_recv()
    y3 = jnp.concatenate([y3_v[i] for i in range(8)], axis=0)

    for a in range(LEAVES):
        cols = slice(a * LEAF, (a + 1) * LEAF)
        far = (times_pair(y3, w_top[a], w_rest[a]) + g_v[a]).astype(BF16)
        far = lax.dot_general(
            far, basis_v[cols, :], (((1,), (1,)), ((), ())), preferred_element_type=F32
        ).astype(BF16)
        for h in range(HIGH):
            mask = mask_v[h, :, cols]
            for i in range(2):
                at = h * COLS + 16 * i
                zs_v[at : at + 16, cols] = far[16 * i : 16 * i + 16] * mask
    def collect(i, carry):
        rows = pl.ds(pl.multiple_of(i * 512, 512), 512)
        total = jnp.dot(zs_v[rows, :], hot_v[...], preferred_element_type=F32)
        for h in range(HIGH):
            cols = pl.ds(pl.multiple_of((i * HIGH + h) * LOW, LOW), LOW)
            out_h[:, cols] += total[h * COLS : (h + 1) * COLS]
        return carry

    lax.fori_loop(0, 1 + w // 32, collect, 0)
    for copy in sends[-7:]:
        copy.wait_send()


def on_device(
    points, leaf_basis, right_sides, leaf_order, local_up, local_down, local_links, upper_nodes
):
    vm = pltpu.VMEM
    dma = pltpu.SemaphoreType.DMA
    scratch = [
        vm((DIMS, PTS), F32),
        vm((PTS, RANK), BF16),
        vm((COLS, PTS), BF16),
        vm((32, 128), jnp.int32),
        vm((14, RANK, RANK), BF16),
        vm((14, RANK, RANK), BF16),
        vm((7, 2, RANK, RANK), BF16),
        vm((8, RANK, RANK), BF16),
        vm((8, 2, RANK, RANK), BF16),
        vm((HIGH * COLS, LOW), BF16),
        vm((PTS, LOW), BF16),
        vm((HIGH, 16, PTS), BF16),
        vm((HIGH * COLS, PTS), BF16),
        vm((COLS, PTS), BF16),
        vm((8, COLS, RANK), F32),
        vm((4, COLS, RANK), F32),
        vm((2, COLS, RANK), F32),
        vm((14, COLS, RANK), F32),
        vm((COLS, RANK), F32),
        vm((COLS, RANK), F32),
        vm((2, 2, 16, RANK), F32),
        vm((3, 8, 4, RANK), F32),
        vm((31, 4, RANK), F32),
        vm((24, 4, RANK), F32),
        vm((6, 16, RANK), F32),
        vm((2, 16, RANK), F32),
        vm((3, 4, RANK), F32),
        vm((7, 4, RANK), F32),
        vm((8, 4, RANK), F32),
        vm((3 * RANK, RANK), BF16),
        vm((3 * RANK, RANK), BF16),
        vm((8, RANK, RANK), BF16),
        vm((8, RANK, RANK), BF16),
        vm((6, RANK, RANK), F32),
        vm((8, COLS, RANK), F32),
        dma((9,)),
        dma((23,)),
        dma((23,)),
        dma,
        dma,
        dma,
        dma,
    ]
    operands = [
        pltpu.with_memory_space_constraint(operand, pltpu.HBM)
        for operand in (
            points, leaf_basis, right_sides, leaf_order.reshape(32, 128), local_up, local_down,
            local_links, upper_nodes.reshape(8, 3, RANK, RANK),
        )
    ]
    return pl.pallas_call(
        kernel,
        out_shape=pltpu.VMEM((COLS, PTS), F32),
        in_specs=[pl.BlockSpec(memory_space=pltpu.HBM)] * 8,
        out_specs=pl.BlockSpec(memory_space=pltpu.VMEM),
        scratch_shapes=scratch,
        compiler_params=pltpu.CompilerParams(
            collective_id=0, has_side_effects=True, vmem_limit_bytes=48 * 2**20
        ),
    )(*operands)


def solution(mesh):
    in_specs = (
        P(None, ("leaf", "wide")),
        P(("leaf", "wide"), None),
        P(None, ("leaf", "wide")),
        P(("leaf", "wide")),
        P(("leaf", "wide"), None, None),
        P(("leaf", "wide"), None, None),
        P(("leaf", "wide"), None, None, None),
        P(("leaf", "wide"), None, None, None, None),
    )
    out_specs = P(None, ("leaf", "wide"))
    return jax.shard_map(
        on_device, mesh=mesh, in_specs=in_specs, out_specs=out_specs, check_vma=False
    )
```
